32 devices in a mesh: dp: 2 (over y), expert: 16 (over z, x, core).
Axes of the slice: x: 2, y: 2, z: 4, core: 2. Of those that a mesh axis runs over, the one named last changes fastest.
Arguments:
- tokens: bfloat16 [512, 2048], P(('dp', 'expert')), may hold values from -6 to 6
- cotangent: bfloat16 [512, 2048], P(('dp', 'expert')), may hold values from -6 to 6
- gate_probs: float32 [512, 8], P(('dp', 'expert')), may hold values from 0.15 to 0.35
- expert_ids: int32 [512, 8], P(('dp', 'expert')), may hold values from 0 to 15, as said below
- up_weight: bfloat16 [16, 768, 2048], P('expert', 'dp'), may hold values from -0.125 to 0.125
- down_weight: bfloat16 [16, 768, 2048], P('expert', 'dp'), may hold values from -0.21875 to 0.21875
Outputs:
- mixture: bfloat16 [512, 2048], P(('dp', 'expert'))
- input_grad: bfloat16 [512, 2048], P(('dp', 'expert'))
- gate_grad: float32 [512, 8], P(('dp', 'expert'))
The draws below stay inside these ranges and needn't reach their ends.
Inputs may be any that keep to these rules, and one draw needn't show every extreme that they name: `expert_ids`: the 8 experts of a row differ. The 16 rows of every device name one and the same expert exactly 9 times; they name every other expert at most 8 times, and one other expert exactly 8 times on every device.
All inputs are finite; a program needn't handle non-finite values.
Results may differ from the reference program's by a relative error of at most 0.0058.
Values may be sent and summed in bfloat16 or wider, within the bound.
A program may use at most 64 MiB of HBM per device.

```python
import jax
import jax.numpy as jnp
from jax import lax

D = 2048
H = 768
TOP = 8
TOK_DEV = 16
EXPERTS = 16
TOKENS = 512
HOTL = 9
CAP = 8
DEVICES = 32


def draw_expert_ids(key, part):
    key = jax.random.fold_in(key, 5)
    cold_total = EXPERTS - 1
    hottest = jax.random.randint(jax.random.fold_in(key, 1), (), 0, EXPERTS)
    filled = jax.random.randint(jax.random.fold_in(key, 2), (), 0, cold_total)
    blocks = TOKENS // TOK_DEV

    def one_block(block_index):
        block_key = jax.random.fold_in(key, block_index + 100)
        row_order = jax.random.permutation(jax.random.fold_in(block_key, 1), TOK_DEV)
        marked = jnp.zeros((TOK_DEV,), jnp.int32).at[row_order[:HOTL]].set(1)
        cold_count = TOP - marked
        offset = jnp.cumsum(cold_count) - cold_count
        column = jnp.arange(TOP, dtype=jnp.int32)
        position = offset[:, None] + column[None, :]
        mixing = jax.random.permutation(jax.random.fold_in(block_key, 2), cold_total)
        leading = mixing[0]
        mixing = jnp.where(mixing == filled, leading, mixing).at[0].set(filled)
        cold_index = mixing[position % cold_total]
        chosen = cold_index + (cold_index >= hottest).astype(jnp.int32)
        picked = jnp.where(column[None, :] < cold_count[:, None], chosen, hottest)
        rotation = jax.random.randint(jax.random.fold_in(block_key, 3), (TOK_DEV,), 0, TOP)
        return jnp.take_along_axis(picked, (column[None, :] + rotation[:, None]) % TOP, axis=1)
    return jax.vmap(one_block)(jnp.arange(blocks)).reshape(TOKENS, TOP).astype(jnp.int32)


def block_scale(rng, dims, split, smallest, high):
    level = 1.0
    for dim, shards_of in split:
        steps = jax.random.uniform(jax.random.fold_in(jax.random.fold_in(rng, 6), dim), (shards_of,), jnp.float32, smallest / len(split), high / len(split))
        level = level * jnp.repeat(jnp.exp(steps), dims[dim] // shards_of).reshape((-1,) + (1,) * (len(dims) - 1 - dim))
    return level


def gaussian(key, dims, deviation, reach, pieces=(), kind=jnp.bfloat16):
    level = block_scale(key, dims, pieces, -0.22, 0.18) if pieces else 1.0
    values = jax.random.normal(key, dims, jnp.float32) * deviation * level
    return jnp.minimum(jnp.maximum(values, -reach), reach).astype(kind)


def setup_inputs(seed: int = 0) -> dict:
    arg_keys = jax.random.split(jax.random.key(seed), 7)
    return {
        "tokens": gaussian(arg_keys[0], (TOKENS, D), 1.0, 6.0, ((0, 32),)),
        "cotangent": gaussian(arg_keys[1], (TOKENS, D), 1.0, 6.0, ((0, 32),)),
        "gate_probs": jnp.clip(0.15 + 0.19999999 * jax.random.uniform(arg_keys[2], (TOKENS, TOP), jnp.float32) ** block_scale(arg_keys[2], (TOKENS, TOP), ((0, 32),), -0.2, 0.2), 0.15, 0.35),
        "expert_ids": draw_expert_ids(jax.random.fold_in(arg_keys[6], 71), 0),
        "up_weight": gaussian(arg_keys[4], (EXPERTS, H, D), D ** -0.5, 0.125, ((0, 16), (1, 2))),
        "down_weight": gaussian(arg_keys[5], (EXPERTS, H, D), H ** -0.5, 0.21875, ((0, 16), (1, 2))),
    }


def expert_terms(features, row_grads, up_part, down_part):
    pre_act = jnp.dot(features, up_part.T, preferred_element_type=jnp.float32)
    gating = jax.nn.sigmoid(pre_act)
    hidden = (pre_act * gating).astype(jnp.bfloat16)
    output_rows = jnp.dot(hidden, down_part, preferred_element_type=jnp.float32)
    hidden_grad = jnp.dot(row_grads, down_part.T, preferred_element_type=jnp.float32)
    act_grad = (hidden_grad * gating * (1.0 + pre_act * (1.0 - gating))).astype(jnp.bfloat16)
    input_rows = jnp.dot(act_grad, up_part, preferred_element_type=jnp.float32)
    return output_rows.astype(jnp.bfloat16), input_rows.astype(jnp.bfloat16)


def reference(tokens, cotangent, gate_probs, expert_ids, up_weight, down_weight):
    flat_ids = expert_ids.reshape(-1).astype(jnp.int32)
    slots_all = flat_ids.shape[0]
    one_hot = (flat_ids[:, None] == jnp.arange(EXPERTS, dtype=jnp.int32)[None, :]).astype(jnp.int32)
    hottest = jnp.argmax(jnp.sum(one_hot, 0)).astype(jnp.int32)
    zero_row = jnp.zeros((1, D), tokens.dtype)
    padded_tokens = jnp.concatenate([tokens, zero_row], 0)
    padded_grads = jnp.concatenate([cotangent, zero_row], 0)
    padded_gates = jnp.concatenate([gate_probs.reshape(-1), jnp.zeros((1,), gate_probs.dtype)], 0)

    def visit(running, expert, row_limit, selected):
        slot_ids = jnp.nonzero(selected, size=row_limit, fill_value=slots_all)[0].astype(jnp.int32)
        row_ids = slot_ids // TOP
        features = padded_tokens[row_ids]
        row_grads = padded_grads[row_ids]
        output_rows, input_rows = expert_terms(features, row_grads, up_weight[expert], down_weight[expert])
        scale = padded_gates[slot_ids][:, None]
        mix_total, grad_total, gate_total = running
        mix_total = mix_total.at[row_ids].add(scale * output_rows.astype(jnp.float32), mode="drop")
        grad_total = grad_total.at[row_ids].add(scale * input_rows.astype(jnp.float32), mode="drop")
        products = jnp.sum(row_grads.astype(jnp.float32) * output_rows.astype(jnp.float32), 1)
        gate_total = gate_total.at[slot_ids].set(products, mode="drop")
        return (mix_total, grad_total, gate_total)

    def cold_step(running, expert):
        selected = jnp.logical_and(flat_ids == expert, expert != hottest)
        return visit(running, expert, CAP * DEVICES, selected), None

    initial = (jnp.zeros((TOKENS, D), jnp.float32), jnp.zeros((TOKENS, D), jnp.float32), jnp.zeros((slots_all,), jnp.float32))
    running, unused = lax.scan(cold_step, initial, jnp.arange(EXPERTS, dtype=jnp.int32))
    running = visit(running, hottest, HOTL * DEVICES, flat_ids == hottest)
    mix_total, grad_total, gate_total = running
    return mix_total.astype(jnp.bfloat16), grad_total.astype(jnp.bfloat16), gate_total.reshape(TOKENS, TOP)
```

```python
import functools

import jax
import jax.numpy as jnp
from jax import lax
from jax.experimental import pallas as pl
from jax.experimental.pallas import tpu as pltpu
from jax.sharding import PartitionSpec as P


def broadcast(block, axis, owner):
    block = jnp.where(lax.axis_index(axis) == owner, block, jnp.zeros_like(block))
    return lax.psum(block, axis)


def expert_terms(row_block, up_piece, down_piece):
    model_width = row_block.shape[1] // 2
    features = row_block[:, :model_width]
    row_grads = row_block[:, model_width:]
    pre_act = jnp.einsum("rd,hd->rh", features, up_piece, preferred_element_type=jnp.float32)
    gating = jax.nn.sigmoid(pre_act)
    hidden = (pre_act * gating).astype(jnp.bfloat16)
    output_rows = jnp.dot(hidden, down_piece, preferred_element_type=jnp.float32)
    hidden_grad = jnp.einsum("rd,hd->rh", row_grads, down_piece, preferred_element_type=jnp.float32)
    act_grad = (hidden_grad * gating * (1.0 + pre_act * (1.0 - gating))).astype(jnp.bfloat16)
    input_rows = jnp.dot(act_grad, up_piece, preferred_element_type=jnp.float32)
    return jnp.concatenate([output_rows, input_rows], 1)


def spread(up_parts, down_parts, row_sets):
    model_width = up_parts.shape[2]
    initial = tuple(
        (jnp.zeros((row_block.shape[0], 2 * model_width), jnp.float32) for row_block in row_sets)
    )
    up_piece = lax.all_gather(up_parts, "dp", axis=1, tiled=True)
    down_piece = lax.all_gather(down_parts, "dp", axis=1, tiled=True)
    return tuple(
        (
            expert_terms(row_block, up_piece[member], down_piece[member])
            for member, (running, row_block) in enumerate(zip(initial, row_sets))
        )
    )


def shards(tokens, cotangent, gate_probs, expert_ids, up_weight, down_weight):
    tok_rows, model_width = tokens.shape
    top_count = expert_ids.shape[1]
    experts = lax.axis_size("expert")
    hot_rows = 9 * tok_rows // 16
    cold_total = experts - 1
    capacity = (tok_rows * top_count - hot_rows + cold_total - 1) // cold_total
    flat_ids = expert_ids.reshape(-1)
    slot_count = flat_ids.shape[0]
    one_hot = (flat_ids[:, None] == jnp.arange(experts, dtype=jnp.int32)[None, :]).astype(jnp.int32)
    hottest = jnp.argmax(jnp.sum(one_hot, 0))
    before = jnp.cumsum(one_hot, 0) - one_hot
    slot_rank = jnp.sum(before * one_hot, 1)
    slot_total = experts * capacity + hot_rows
    slot_index = jnp.where(
        flat_ids == hottest, experts * capacity + slot_rank, flat_ids * capacity + slot_rank
    )
    source_slot = (
        jnp.full((slot_total,), slot_count, jnp.int32)
        .at[slot_index]
        .set(jnp.arange(slot_count, dtype=jnp.int32))
    )
    source_row = source_slot // top_count
    payload = jnp.concatenate([tokens, cotangent], 1)
    padded_payload = jnp.concatenate([payload, jnp.zeros((1, 2 * model_width), payload.dtype)], 0)
    placed = padded_payload[source_row]
    outgoing = placed[: experts * capacity].reshape(experts, capacity, 2 * model_width)
    local_rows = placed[experts * capacity :]
    arrived = lax.all_to_all(outgoing, "expert", split_axis=0, concat_axis=0, tiled=True)
    arrived_rows = arrived.reshape(experts * capacity, 2 * model_width)
    shadow_up, shadow_down = (
        broadcast(up_weight[0], "expert", hottest),
        broadcast(down_weight[0], "expert", hottest),
    )
    (own_out,) = spread(up_weight, down_weight, [arrived_rows])
    (hot_out,) = spread(shadow_up[None], shadow_down[None], [local_rows])
    returning = own_out.astype(jnp.bfloat16).reshape(experts, capacity, 2 * model_width)
    came_back = lax.all_to_all(returning, "expert", split_axis=0, concat_axis=0, tiled=True)
    results = jnp.concatenate(
        [came_back.reshape(experts * capacity, 2 * model_width), hot_out.astype(jnp.bfloat16)], 0
    )
    per_slot = results[slot_index].astype(jnp.float32).reshape(tok_rows, top_count, 2 * model_width)
    scale = gate_probs[:, :, None]
    mixture = jnp.sum(scale * per_slot[:, :, :model_width], 1).astype(jnp.bfloat16)
    input_grad = jnp.sum(scale * per_slot[:, :, model_width:], 1).astype(jnp.bfloat16)
    gate_grad = jnp.sum(cotangent.astype(jnp.float32)[:, None, :] * per_slot[:, :, :model_width], 2)
    return (mixture, input_grad, gate_grad)


MESH = pl.DeviceIdType.MESH
LANES = 128
Z, Y, X, C = 4, 2, 2, 2


def exchange_kernel(
    experts,
    tokens_ref, cotangent_ref, gate_ref, ids_ref, up_hbm, down_hbm,
    mixture_ref, input_grad_ref, gate_grad_ref,
    up, down, gathered, partial, from_core, core_sum, from_first, first_sum, from_second, plane_sum, from_z,
    load_sem, send_sem, recv_sem,
):
    width = tokens_ref.shape[1]
    near = LANES + width
    rows = tokens_ref.shape[0]
    y, expert = lax.axis_index("dp"), lax.axis_index("expert")
    z = expert // (X * C)
    x = (expert // C) % X
    c = expert % C
    far_y, far_x, far_c = 1 - y, 1 - x, 1 - c

    def place(yy, zz, xx, cc):
        return (yy, (zz * X + xx) * C + cc)

    by_x, by_y, by_c = place(y, z, far_x, c), place(far_y, z, x, c), place(y, z, x, far_c)
    planes = [(z + step) % Z for step in range(Z)]

    loads = [
        pltpu.make_async_copy(up_hbm.at[0], up, load_sem.at[0]),
        pltpu.make_async_copy(down_hbm.at[0], down, load_sem.at[1]),
    ]
    for load in loads:
        load.start()

    barrier = pltpu.get_barrier_semaphore()
    partners = [by_x, by_y, by_c] + [place(y, planes[step], x, c) for step in range(1, Z)]
    for partner in partners:
        pl.semaphore_signal(barrier, inc=1, device_id=partner, device_id_type=MESH)

    lane = lax.broadcasted_iota(jnp.int32, (rows, LANES), 1)
    weights = jnp.zeros((rows, LANES), jnp.float32)
    for k in range(gate_ref.shape[1]):
        weights += jnp.where(lane == ids_ref[:, k : k + 1], gate_ref[:, k : k + 1], 0.0)
    high = weights.astype(jnp.bfloat16).astype(jnp.float32)
    rest = jnp.zeros((rows, LANES), jnp.float32)
    for k in range(gate_ref.shape[1]):
        gate = gate_ref[:, k : k + 1]
        rest += jnp.where(
            lane == ids_ref[:, k : k + 1] + experts,
            gate - gate.astype(jnp.bfloat16).astype(jnp.float32),
            0.0,
        )
    gathered[0, c, y, x, :, :LANES] = (high + rest).astype(jnp.bfloat16)
    gathered[0, c, y, x, :, LANES:near] = tokens_ref[...]
    gathered[0, c, y, x, :, near:] = cotangent_ref[...]
    pl.semaphore_wait(barrier, len(partners))

    started = []

    def send(src, dst, device):
        index = len(started)
        copy = pltpu.make_async_remote_copy(
            src_ref=src, dst_ref=dst, send_sem=send_sem.at[index], recv_sem=recv_sem.at[index],
            device_id=device, device_id_type=MESH,
        )
        copy.start()
        started.append(copy)
        return copy

    first_cols, second_cols = pl.ds(0, near), pl.ds(near, width)
    pending = {}
    for step in range(1, Z):
        src = gathered.at[0, c, y, x]
        pending["z", Z - step] = send(src, gathered.at[Z - step, c, y, x], place(y, planes[step], x, c))

    def gather_first(j):
        if j:
            pending["z", j].wait_recv()
        for name, cols, device in (("fa", first_cols, by_x), ("fb", second_cols, by_y)):
            ref = gathered.at[j, c, y, x, :, cols]
            pending[name, j] = send(ref, ref, device)

    def gather_second(j):
        pending["fa", j].wait_recv()
        ref = gathered.at[j, c, y, :, :, first_cols]
        pending["sa", j] = send(ref, ref, by_y)
        pending["fb", j].wait_recv()
        ref = gathered.at[j, c, :, x, :, second_cols]
        pending["sb", j] = send(ref, ref, by_x)

    def gather_core(j):
        pending["sa", j].wait_recv()
        pending["sb", j].wait_recv()
        ref = gathered.at[j, c]
        pending["c", j] = send(ref, ref, by_c)

    def evaluate(j):
        pending["c", j].wait_recv()
        if j == 0:
            for load in loads:
                load.wait()
        group = C * Y * X * rows
        features = gathered[j, :, :, :, :, LANES:near].reshape(group, width)
        row_grads = gathered[j, :, :, :, :, near:].reshape(group, width)
        extra = gathered[j, :, :, :, :, :LANES].reshape(group, LANES).astype(jnp.float32)
        lanes = lax.broadcasted_iota(jnp.int32, (group, LANES), 1)
        mine = lanes == expert
        weight = jnp.sum(jnp.where(mine | (lanes == expert + experts), extra, 0.0), 1, keepdims=True)
        contract = (((1,), (1,)), ((), ()))
        pre_act = lax.dot_general(features, up[...], contract, preferred_element_type=jnp.float32)
        gating = jax.nn.sigmoid(pre_act)
        hidden = (pre_act * gating).astype(jnp.bfloat16)
        hidden_grad = lax.dot_general(row_grads, down[...], contract, preferred_element_type=jnp.float32)
        act_grad = (hidden_grad * gating * (1.0 + pre_act * (1.0 - gating))).astype(jnp.bfloat16)
        products = jnp.sum(hidden.astype(jnp.float32) * hidden_grad, 1, keepdims=True)
        partial[j, :, :, :, :, :LANES] = (
            jnp.where(mine, products, 0.0).astype(jnp.bfloat16).reshape(C, Y, X, rows, LANES)
        )
        tile = min(512, width)
        for left, matrix, base in ((hidden, down, LANES), (act_grad, up, near)):
            for at in range(0, width, tile):
                result = jnp.dot(left, matrix[:, at : at + tile], preferred_element_type=jnp.float32)
                partial[j, :, :, :, :, base + at : base + at + tile] = (
                    (result * weight).astype(jnp.bfloat16).reshape(C, Y, X, rows, tile)
                )
        pending["rc", j] = send(partial.at[j, far_c], from_core.at[j], by_c)

    def add(one, other):
        return (one.astype(jnp.float32) + other.astype(jnp.float32)).astype(jnp.bfloat16)

    def reduce_first(j):
        pending["rc", j].wait_recv()
        core_sum[j] = add(partial[j, c], from_core[j])
        pending["ra", j] = send(
            core_sum.at[j, far_y, :, :, first_cols], from_first.at[j, :, :, first_cols], by_y
        )
        pending["rb", j] = send(
            core_sum.at[j, :, far_x, :, second_cols], from_first.at[j, :, :, second_cols], by_x
        )

    def reduce_second(j):
        pending["ra", j].wait_recv()
        first_sum[j, :, :, :near] = add(core_sum[j, y, :, :, :near], from_first[j, :, :, :near])
        pending["sra", j] = send(
            first_sum.at[j, far_x, :, first_cols], from_second.at[j, :, first_cols], by_x
        )
        pending["rb", j].wait_recv()
        for yy in range(Y):
            first_sum[j, yy, :, near:] = add(core_sum[j, yy, x, :, near:], from_first[j, yy, :, near:])
        pending["srb", j] = send(
            first_sum.at[j, far_y, :, second_cols], from_second.at[j, :, second_cols], by_y
        )

    def reduce_plane(j):
        pending["sra", j].wait_recv()
        pending["srb", j].wait_recv()
        plane_sum[j, :, :near] = add(first_sum[j, x, :, :near], from_second[j, :, :near])
        plane_sum[j, :, near:] = add(first_sum[j, y, :, near:], from_second[j, :, near:])
        if j:
            pending["rz", j] = send(plane_sum.at[j], from_z.at[j], place(y, planes[j], x, c))

    stages = (
        gather_first, gather_second, gather_core, evaluate, reduce_first, reduce_second, reduce_plane
    )
    for slot in range(len(stages) + Z - 1):
        for j in range(Z):
            if 0 <= slot - j < len(stages):
                stages[slot - j](j)

    total = plane_sum[0].astype(jnp.float32)
    for j in range(1, Z):
        pending["rz", j].wait_recv()
        total += from_z[j].astype(jnp.float32)
    mixture_ref[...] = total[:, LANES:near].astype(jnp.bfloat16)
    input_grad_ref[...] = total[:, near:].astype(jnp.bfloat16)
    per_expert = total[:, :LANES]
    slots = gate_ref.shape[1]
    column = lax.broadcasted_iota(jnp.int32, (rows, slots), 1)
    gate_grad = jnp.zeros((rows, slots), jnp.float32)
    for k in range(slots):
        value = jnp.sum(jnp.where(lane == ids_ref[:, k : k + 1], per_expert, 0.0), 1, keepdims=True)
        gate_grad += jnp.where(column == k, value, 0.0)
    gate_grad_ref[...] = gate_grad
    for copy in started:
        copy.wait_send()


def token_shards(tokens, cotangent, gate_probs, expert_ids, up_weight, down_weight):
    rows, width = tokens.shape
    experts = lax.axis_size("expert")
    hidden_part = up_weight.shape[1]
    wide = LANES + 2 * width
    kind = jnp.bfloat16
    copies = 2 * (Z - 1) + 11 * Z
    vmem = pl.BlockSpec(memory_space=pltpu.VMEM)
    hbm = pl.BlockSpec(memory_space=pl.ANY)
    return tuple(pl.pallas_call(
        functools.partial(exchange_kernel, experts),
        out_shape=(
            jax.ShapeDtypeStruct((rows, width), kind),
            jax.ShapeDtypeStruct((rows, width), kind),
            jax.ShapeDtypeStruct(gate_probs.shape, jnp.float32),
        ),
        in_specs=[vmem, vmem, vmem, vmem, hbm, hbm],
        out_specs=(vmem, vmem, vmem),
        scratch_shapes=[
            pltpu.VMEM((hidden_part, width), kind),
            pltpu.VMEM((hidden_part, width), kind),
            pltpu.VMEM((Z, C, Y, X, rows, wide), kind),
            pltpu.VMEM((Z, C, Y, X, rows, wide), kind),
            pltpu.VMEM((Z, Y, X, rows, wide), kind),
            pltpu.VMEM((Z, Y, X, rows, wide), kind),
            pltpu.VMEM((Z, 2, rows, wide), kind),
            pltpu.VMEM((Z, 2, rows, wide), kind),
            pltpu.VMEM((Z, rows, wide), kind),
            pltpu.VMEM((Z, rows, wide), kind),
            pltpu.VMEM((Z, rows, wide), kind),
            pltpu.SemaphoreType.DMA((2,)),
            pltpu.SemaphoreType.DMA((copies,)),
            pltpu.SemaphoreType.DMA((copies,)),
        ],
        compiler_params=pltpu.CompilerParams(
            collective_id=0, has_side_effects=True, vmem_limit_bytes=48 * 1024 * 1024
        ),
    )(tokens, cotangent, gate_probs, expert_ids, up_weight, down_weight))


def solution(mesh):
    small = dict(mesh.shape) == {"dp": Y, "expert": Z * X * C}
    placed = (
        P(("dp", "expert"), None),
        P(("dp", "expert"), None),
        P(("dp", "expert"), None),
        P(("dp", "expert"), None),
        P("expert", "dp", None),
        P("expert", "dp", None),
    )
    return jax.shard_map(
        token_shards if small else shards,
        mesh=mesh,
        in_specs=placed,
        out_specs=(P(("dp", "expert"), None), P(("dp", "expert"), None), P(("dp", "expert"), None)),
        check_vma=False,
    )
```

```python
import functools

import jax
import jax.numpy as jnp
from jax import lax
from jax.experimental import pallas as pl
from jax.experimental.pallas import tpu as pltpu
from jax.sharding import PartitionSpec as P


def broadcast(block, axis, owner):
    block = jnp.where(lax.axis_index(axis) == owner, block, jnp.zeros_like(block))
    return lax.psum(block, axis)


def expert_terms(row_block, up_piece, down_piece):
    model_width = row_block.shape[1] // 2
    features = row_block[:, :model_width]
    row_grads = row_block[:, model_width:]
    pre_act = jnp.einsum("rd,hd->rh", features, up_piece, preferred_element_type=jnp.float32)
    gating = jax.nn.sigmoid(pre_act)
    hidden = (pre_act * gating).astype(jnp.bfloat16)
    output_rows = jnp.dot(hidden, down_piece, preferred_element_type=jnp.float32)
    hidden_grad = jnp.einsum("rd,hd->rh", row_grads, down_piece, preferred_element_type=jnp.float32)
    act_grad = (hidden_grad * gating * (1.0 + pre_act * (1.0 - gating))).astype(jnp.bfloat16)
    input_rows = jnp.dot(act_grad, up_piece, preferred_element_type=jnp.float32)
    return jnp.concatenate([output_rows, input_rows], 1)


def spread(up_parts, down_parts, row_sets):
    model_width = up_parts.shape[2]
    initial = tuple(
        (jnp.zeros((row_block.shape[0], 2 * model_width), jnp.float32) for row_block in row_sets)
    )
    up_piece = lax.all_gather(up_parts, "dp", axis=1, tiled=True)
    down_piece = lax.all_gather(down_parts, "dp", axis=1, tiled=True)
    return tuple(
        (
            expert_terms(row_block, up_piece[member], down_piece[member])
            for member, (running, row_block) in enumerate(zip(initial, row_sets))
        )
    )


def shards(tokens, cotangent, gate_probs, expert_ids, up_weight, down_weight):
    tok_rows, model_width = tokens.shape
    top_count = expert_ids.shape[1]
    experts = lax.axis_size("expert")
    hot_rows = 9 * tok_rows // 16
    cold_total = experts - 1
    capacity = (tok_rows * top_count - hot_rows + cold_total - 1) // cold_total
    flat_ids = expert_ids.reshape(-1)
    slot_count = flat_ids.shape[0]
    one_hot = (flat_ids[:, None] == jnp.arange(experts, dtype=jnp.int32)[None, :]).astype(jnp.int32)
    hottest = jnp.argmax(jnp.sum(one_hot, 0))
    before = jnp.cumsum(one_hot, 0) - one_hot
    slot_rank = jnp.sum(before * one_hot, 1)
    slot_total = experts * capacity + hot_rows
    slot_index = jnp.where(
        flat_ids == hottest, experts * capacity + slot_rank, flat_ids * capacity + slot_rank
    )
    source_slot = (
        jnp.full((slot_total,), slot_count, jnp.int32)
        .at[slot_index]
        .set(jnp.arange(slot_count, dtype=jnp.int32))
    )
    source_row = source_slot // top_count
    payload = jnp.concatenate([tokens, cotangent], 1)
    padded_payload = jnp.concatenate([payload, jnp.zeros((1, 2 * model_width), payload.dtype)], 0)
    placed = padded_payload[source_row]
    outgoing = placed[: experts * capacity].reshape(experts, capacity, 2 * model_width)
    local_rows = placed[experts * capacity :]
    arrived = lax.all_to_all(outgoing, "expert", split_axis=0, concat_axis=0, tiled=True)
    arrived_rows = arrived.reshape(experts * capacity, 2 * model_width)
    shadow_up, shadow_down = (
        broadcast(up_weight[0], "expert", hottest),
        broadcast(down_weight[0], "expert", hottest),
    )
    (own_out,) = spread(up_weight, down_weight, [arrived_rows])
    (hot_out,) = spread(shadow_up[None], shadow_down[None], [local_rows])
    returning = own_out.astype(jnp.bfloat16).reshape(experts, capacity, 2 * model_width)
    came_back = lax.all_to_all(returning, "expert", split_axis=0, concat_axis=0, tiled=True)
    results = jnp.concatenate(
        [came_back.reshape(experts * capacity, 2 * model_width), hot_out.astype(jnp.bfloat16)], 0
    )
    per_slot = results[slot_index].astype(jnp.float32).reshape(tok_rows, top_count, 2 * model_width)
    scale = gate_probs[:, :, None]
    mixture = jnp.sum(scale * per_slot[:, :, :model_width], 1).astype(jnp.bfloat16)
    input_grad = jnp.sum(scale * per_slot[:, :, model_width:], 1).astype(jnp.bfloat16)
    gate_grad = jnp.sum(cotangent.astype(jnp.float32)[:, None, :] * per_slot[:, :, :model_width], 2)
    return (mixture, input_grad, gate_grad)


MESH = pl.DeviceIdType.MESH
LANES = 128
Z, Y, X, C = 4, 2, 2, 2


def exchange_kernel(
    experts,
    tokens_hbm, cotangent_hbm, gate_ref, ids_ref, up_hbm, down_hbm,
    mixture_ref, input_grad_ref, gate_grad_ref,
    up, down, gathered, partial, from_core, core_sum, from_first, first_sum, from_second, plane_sum, from_z,
    load_sem, send_sem, recv_sem,
):
    width = tokens_hbm.shape[1]
    near = LANES + width
    rows = tokens_hbm.shape[0]
    y, expert = lax.axis_index("dp"), lax.axis_index("expert")
    z = expert // (X * C)
    x = (expert // C) % X
    c = expert % C
    far_y, far_x, far_c = 1 - y, 1 - x, 1 - c

    def place(yy, zz, xx, cc):
        return (yy, (zz * X + xx) * C + cc)

    by_x, by_y, by_c = place(y, z, far_x, c), place(far_y, z, x, c), place(y, z, x, far_c)
    planes = [z, z + 1 - 2 * (z % 2), (z + 2) % Z, Z - 1 - z]

    loads = [
        pltpu.make_async_copy(tokens_hbm, gathered.at[0, c, y, x, :, pl.ds(LANES, width)], load_sem.at[0]),
        pltpu.make_async_copy(cotangent_hbm, gathered.at[0, c, y, x, :, pl.ds(near, width)], load_sem.at[1]),
        pltpu.make_async_copy(up_hbm.at[0], up, load_sem.at[2]),
        pltpu.make_async_copy(down_hbm.at[0], down, load_sem.at[3]),
    ]
    for load in loads:
        load.start()

    barrier = pltpu.get_barrier_semaphore()
    partners = [by_x, by_y, by_c] + [place(y, planes[step], x, c) for step in range(1, Z)]
    for partner in partners:
        pl.semaphore_signal(barrier, inc=1, device_id=partner, device_id_type=MESH)

    slots = gate_ref.shape[0]
    names = lax.broadcasted_iota(jnp.int32, (LANES, rows), 0)
    weights = jnp.zeros((LANES, rows), jnp.float32)
    for k in range(slots):
        gate, chosen = gate_ref[k : k + 1, :], ids_ref[k : k + 1, :]
        high = gate.astype(jnp.bfloat16).astype(jnp.float32)
        weights += jnp.where(names == chosen, high, 0.0)
        weights += jnp.where(names == chosen + experts, gate - high, 0.0)
    square = (rows, rows)
    diagonal = lax.broadcasted_iota(jnp.int32, square, 0) == lax.broadcasted_iota(jnp.int32, square, 1)
    turned = lax.dot_general(
        jnp.where(diagonal, 1.0, 0.0).astype(jnp.bfloat16), weights.astype(jnp.bfloat16),
        (((1,), (1,)), ((), ())), preferred_element_type=jnp.float32,
    )
    gathered[0, c, y, x, :, :LANES] = turned.astype(jnp.bfloat16)
    loads[0].wait()
    loads[1].wait()
    pl.semaphore_wait(barrier, len(partners))

    started = []

    def send(src, dst, device):
        index = len(started)
        copy = pltpu.make_async_remote_copy(
            src_ref=src, dst_ref=dst, send_sem=send_sem.at[index], recv_sem=recv_sem.at[index],
            device_id=device, device_id_type=MESH,
        )
        copy.start()
        started.append(copy)
        return copy

    first_cols, second_cols = pl.ds(0, near), pl.ds(near, width)
    pending = {}

    def send_plane(j):
        src = gathered.at[0, c, y, x]
        pending["z", j] = send(src, gathered.at[j, c, y, x], place(y, planes[j], x, c))

    def gather_first(j):
        if j:
            pending["z", j].wait_recv()
        for name, cols, device in (("fa", first_cols, by_x), ("fb", second_cols, by_y)):
            ref = gathered.at[j, c, y, x, :, cols]
            pending[name, j] = send(ref, ref, device)

    def gather_second(j):
        pending["fa", j].wait_recv()
        ref = gathered.at[j, c, y, :, :, first_cols]
        pending["sa", j] = send(ref, ref, by_y)
        pending["fb", j].wait_recv()
        ref = gathered.at[j, c, :, x, :, second_cols]
        pending["sb", j] = send(ref, ref, by_x)

    def gather_core(j):
        pending["sa", j].wait_recv()
        pending["sb", j].wait_recv()
        ref = gathered.at[j, c]
        pending["c", j] = send(ref, ref, by_c)

    def evaluate(j):
        pending["c", j].wait_recv()
        if j == 0:
            loads[2].wait()
            loads[3].wait()
        group = C * Y * X * rows
        features = gathered[j, :, :, :, :, LANES:near].reshape(group, width)
        row_grads = gathered[j, :, :, :, :, near:].reshape(group, width)
        extra = gathered[j, :, :, :, :, :LANES].reshape(group, LANES).astype(jnp.float32)
        lanes = lax.broadcasted_iota(jnp.int32, (group, LANES), 1)
        mine = lanes == expert
        weight = jnp.sum(jnp.where(mine | (lanes == expert + experts), extra, 0.0), 1, keepdims=True)
        contract = (((1,), (1,)), ((), ()))
        pre_act = lax.dot_general(features, up[...], contract, preferred_element_type=jnp.float32)
        gating = jax.nn.sigmoid(pre_act)
        hidden = (pre_act * gating).astype(jnp.bfloat16)
        hidden_grad = lax.dot_general(row_grads, down[...], contract, preferred_element_type=jnp.float32)
        act_grad = (hidden_grad * gating * (1.0 + pre_act * (1.0 - gating))).astype(jnp.bfloat16)
        products = jnp.sum(hidden.astype(jnp.float32) * hidden_grad, 1, keepdims=True)
        partial[j, :, :, :, :, :LANES] = (
            jnp.where(mine, products, 0.0).astype(jnp.bfloat16).reshape(C, Y, X, rows, LANES)
        )
        tile = min(512, width)
        for left, matrix, base in ((hidden, down, LANES), (act_grad, up, near)):
            for at in range(0, width, tile):
                result = jnp.dot(left, matrix[:, at : at + tile], preferred_element_type=jnp.float32)
                partial[j, :, :, :, :, base + at : base + at + tile] = (
                    (result * weight).astype(jnp.bfloat16).reshape(C, Y, X, rows, tile)
                )
        pending["rc", j] = send(partial.at[j, far_c], from_core.at[j], by_c)

    def add(one, other):
        return (one.astype(jnp.float32) + other.astype(jnp.float32)).astype(jnp.bfloat16)

    def reduce_first(j):
        pending["rc", j].wait_recv()
        core_sum[j] = add(partial[j, c], from_core[j])
        pending["ra", j] = send(
            core_sum.at[j, far_y, :, :, first_cols], from_first.at[j, :, :, first_cols], by_y
        )
        pending["rb", j] = send(
            core_sum.at[j, :, far_x, :, second_cols], from_first.at[j, :, :, second_cols], by_x
        )

    def reduce_second(j):
        pending["ra", j].wait_recv()
        first_sum[j, :, :, :near] = add(core_sum[j, y, :, :, :near], from_first[j, :, :, :near])
        pending["sra", j] = send(
            first_sum.at[j, far_x, :, first_cols], from_second.at[j, :, first_cols], by_x
        )
        pending["rb", j].wait_recv()
        for yy in range(Y):
            first_sum[j, yy, :, near:] = add(core_sum[j, yy, x, :, near:], from_first[j, yy, :, near:])
        pending["srb", j] = send(
            first_sum.at[j, far_y, :, second_cols], from_second.at[j, :, second_cols], by_y
        )

    def reduce_plane(j):
        pending["sra", j].wait_recv()
        pending["srb", j].wait_recv()
        plane_sum[j, :, :near] = add(first_sum[j, x, :, :near], from_second[j, :, :near])
        plane_sum[j, :, near:] = add(first_sum[j, y, :, near:], from_second[j, :, near:])
        if j:
            pending["rz", j] = send(plane_sum.at[j], from_z.at[j], place(y, planes[j], x, c))

    order = (
        (send_plane, 1), (gather_first, 0), (send_plane, 2),
        (gather_second, 0), (gather_first, 1), (send_plane, 3), (gather_core, 0),
        (gather_second, 1), (gather_first, 2), (evaluate, 0),
        (gather_core, 1), (gather_second, 2), (gather_first, 3), (evaluate, 1),
        (gather_core, 2), (gather_second, 3), (reduce_first, 1), (evaluate, 2),
        (gather_core, 3), (reduce_second, 1), (reduce_first, 2), (evaluate, 3),
        (reduce_first, 0), (reduce_plane, 1), (reduce_second, 2), (reduce_first, 3),
        (reduce_second, 0), (reduce_plane, 2), (reduce_second, 3), (reduce_plane, 3), (reduce_plane, 0),
    )
    for stage, j in order:
        stage(j)

    total = plane_sum[0].astype(jnp.float32)
    for j in range(1, Z):
        pending["rz", j].wait_recv()
        total += from_z[j].astype(jnp.float32)
    mixture_ref[...] = total[:, LANES:near].astype(jnp.bfloat16)
    input_grad_ref[...] = total[:, near:].astype(jnp.bfloat16)
    per_expert = lax.dot_general(
        total[:, :LANES], jnp.where(diagonal, 1.0, 0.0), (((0,), (0,)), ((), ())),
        precision=lax.Precision.HIGHEST, preferred_element_type=jnp.float32,
    )
    for k in range(slots):
        gate_grad_ref[k : k + 1, :] = jnp.sum(
            jnp.where(names == ids_ref[k : k + 1, :], per_expert, 0.0), 0, keepdims=True
        )
    for copy in started:
        copy.wait_send()


def token_shards(tokens, cotangent, gate_probs, expert_ids, up_weight, down_weight):
    rows, width = tokens.shape
    experts = lax.axis_size("expert")
    hidden_part = up_weight.shape[1]
    wide = LANES + 2 * width
    kind = jnp.bfloat16
    copies = 2 * (Z - 1) + 11 * Z
    vmem = pl.BlockSpec(memory_space=pltpu.VMEM)
    hbm = pl.BlockSpec(memory_space=pl.ANY)
    mixture, input_grad, gate_grad = pl.pallas_call(
        functools.partial(exchange_kernel, experts),
        out_shape=(
            jax.ShapeDtypeStruct((rows, width), kind),
            jax.ShapeDtypeStruct((rows, width), kind),
            jax.ShapeDtypeStruct(gate_probs.shape[::-1], jnp.float32),
        ),
        in_specs=[hbm, hbm, vmem, vmem, hbm, hbm],
        out_specs=(vmem, vmem, vmem),
        scratch_shapes=[
            pltpu.VMEM((hidden_part, width), kind),
            pltpu.VMEM((hidden_part, width), kind),
            pltpu.VMEM((Z, C, Y, X, rows, wide), kind),
            pltpu.VMEM((Z, C, Y, X, rows, wide), kind),
            pltpu.VMEM((Z, Y, X, rows, wide), kind),
            pltpu.VMEM((Z, Y, X, rows, wide), kind),
            pltpu.VMEM((Z, 2, rows, wide), kind),
            pltpu.VMEM((Z, 2, rows, wide), kind),
            pltpu.VMEM((Z, rows, wide), kind),
            pltpu.VMEM((Z, rows, wide), kind),
            pltpu.VMEM((Z, rows, wide), kind),
            pltpu.SemaphoreType.DMA((4,)),
            pltpu.SemaphoreType.DMA((copies,)),
            pltpu.SemaphoreType.DMA((copies,)),
        ],
        compiler_params=pltpu.CompilerParams(
            collective_id=0, has_side_effects=True, vmem_limit_bytes=60 * 1024 * 1024
        ),
    )(tokens, cotangent, gate_probs.T, expert_ids.T, up_weight, down_weight)
    return mixture, input_grad, gate_grad.T


def solution(mesh):
    small = dict(mesh.shape) == {"dp": Y, "expert": Z * X * C}
    placed = (
        P(("dp", "expert"), None),
        P(("dp", "expert"), None),
        P(("dp", "expert"), None),
        P(("dp", "expert"), None),
        P("expert", "dp", None),
        P("expert", "dp", None),
    )
    return jax.shard_map(
        token_shards if small else shards,
        mesh=mesh,
        in_specs=placed,
        out_specs=(P(("dp", "expert"), None), P(("dp", "expert"), None), P(("dp", "expert"), None)),
        check_vma=False,
    )
```

```python
import functools

import jax
import jax.numpy as jnp
from jax import lax
from jax.experimental import pallas as pl
from jax.experimental.pallas import tpu as pltpu
from jax.sharding import PartitionSpec as P


def broadcast(block, axis, owner):
    block = jnp.where(lax.axis_index(axis) == owner, block, jnp.zeros_like(block))
    return lax.psum(block, axis)


def expert_terms(row_block, up_piece, down_piece):
    model_width = row_block.shape[1] // 2
    features = row_block[:, :model_width]
    row_grads = row_block[:, model_width:]
    pre_act = jnp.einsum("rd,hd->rh", features, up_piece, preferred_element_type=jnp.float32)
    gating = jax.nn.sigmoid(pre_act)
    hidden = (pre_act * gating).astype(jnp.bfloat16)
    output_rows = jnp.dot(hidden, down_piece, preferred_element_type=jnp.float32)
    hidden_grad = jnp.einsum("rd,hd->rh", row_grads, down_piece, preferred_element_type=jnp.float32)
    act_grad = (hidden_grad * gating * (1.0 + pre_act * (1.0 - gating))).astype(jnp.bfloat16)
    input_rows = jnp.dot(act_grad, up_piece, preferred_element_type=jnp.float32)
    return jnp.concatenate([output_rows, input_rows], 1)


def spread(up_parts, down_parts, row_sets):
    model_width = up_parts.shape[2]
    initial = tuple(
        (jnp.zeros((row_block.shape[0], 2 * model_width), jnp.float32) for row_block in row_sets)
    )
    up_piece = lax.all_gather(up_parts, "dp", axis=1, tiled=True)
    down_piece = lax.all_gather(down_parts, "dp", axis=1, tiled=True)
    return tuple(
        (
            expert_terms(row_block, up_piece[member], down_piece[member])
            for member, (running, row_block) in enumerate(zip(initial, row_sets))
        )
    )


def shards(tokens, cotangent, gate_probs, expert_ids, up_weight, down_weight):
    tok_rows, model_width = tokens.shape
    top_count = expert_ids.shape[1]
    experts = lax.axis_size("expert")
    hot_rows = 9 * tok_rows // 16
    cold_total = experts - 1
    capacity = (tok_rows * top_count - hot_rows + cold_total - 1) // cold_total
    flat_ids = expert_ids.reshape(-1)
    slot_count = flat_ids.shape[0]
    one_hot = (flat_ids[:, None] == jnp.arange(experts, dtype=jnp.int32)[None, :]).astype(jnp.int32)
    hottest = jnp.argmax(jnp.sum(one_hot, 0))
    before = jnp.cumsum(one_hot, 0) - one_hot
    slot_rank = jnp.sum(before * one_hot, 1)
    slot_total = experts * capacity + hot_rows
    slot_index = jnp.where(
        flat_ids == hottest, experts * capacity + slot_rank, flat_ids * capacity + slot_rank
    )
    source_slot = (
        jnp.full((slot_total,), slot_count, jnp.int32)
        .at[slot_index]
        .set(jnp.arange(slot_count, dtype=jnp.int32))
    )
    source_row = source_slot // top_count
    payload = jnp.concatenate([tokens, cotangent], 1)
    padded_payload = jnp.concatenate([payload, jnp.zeros((1, 2 * model_width), payload.dtype)], 0)
    placed = padded_payload[source_row]
    outgoing = placed[: experts * capacity].reshape(experts, capacity, 2 * model_width)
    local_rows = placed[experts * capacity :]
    arrived = lax.all_to_all(outgoing, "expert", split_axis=0, concat_axis=0, tiled=True)
    arrived_rows = arrived.reshape(experts * capacity, 2 * model_width)
    shadow_up, shadow_down = (
        broadcast(up_weight[0], "expert", hottest),
        broadcast(down_weight[0], "expert", hottest),
    )
    (own_out,) = spread(up_weight, down_weight, [arrived_rows])
    (hot_out,) = spread(shadow_up[None], shadow_down[None], [local_rows])
    returning = own_out.astype(jnp.bfloat16).reshape(experts, capacity, 2 * model_width)
    came_back = lax.all_to_all(returning, "expert", split_axis=0, concat_axis=0, tiled=True)
    results = jnp.concatenate(
        [came_back.reshape(experts * capacity, 2 * model_width), hot_out.astype(jnp.bfloat16)], 0
    )
    per_slot = results[slot_index].astype(jnp.float32).reshape(tok_rows, top_count, 2 * model_width)
    scale = gate_probs[:, :, None]
    mixture = jnp.sum(scale * per_slot[:, :, :model_width], 1).astype(jnp.bfloat16)
    input_grad = jnp.sum(scale * per_slot[:, :, model_width:], 1).astype(jnp.bfloat16)
    gate_grad = jnp.sum(cotangent.astype(jnp.float32)[:, None, :] * per_slot[:, :, :model_width], 2)
    return (mixture, input_grad, gate_grad)


MESH = pl.DeviceIdType.MESH
LANES = 128
Z, Y, X, C = 4, 2, 2, 2


def exchange_kernel(
    experts,
    tokens_hbm, cotangent_hbm, gate_ref, ids_ref, up_hbm, down_hbm,
    mixture_ref, input_grad_ref, gate_grad_ref,
    up, down, gathered, partial, from_core, core_sum, from_first, first_sum, from_second, plane_sum, from_z,
    load_sem, send_sem, recv_sem,
):
    width = tokens_hbm.shape[1]
    near = LANES + width
    rows = tokens_hbm.shape[0]
    y, expert = lax.axis_index("dp"), lax.axis_index("expert")
    z = expert // (X * C)
    x = (expert // C) % X
    c = expert % C
    far_y, far_x, far_c = 1 - y, 1 - x, 1 - c

    def place(yy, zz, xx, cc):
        return (yy, (zz * X + xx) * C + cc)

    by_x, by_y, by_c = place(y, z, far_x, c), place(far_y, z, x, c), place(y, z, x, far_c)
    planes = [z, z + 1 - 2 * (z % 2), Z - 1 - z, (z + 2) % Z]
    inner = z % (Z - 1) > 0

    loads = [
        pltpu.make_async_copy(tokens_hbm, gathered.at[0, c, y, x, :, pl.ds(LANES, width)], load_sem.at[0]),
        pltpu.make_async_copy(cotangent_hbm, gathered.at[0, c, y, x, :, pl.ds(near, width)], load_sem.at[1]),
        pltpu.make_async_copy(up_hbm.at[0], up, load_sem.at[2]),
        pltpu.make_async_copy(down_hbm.at[0], down, load_sem.at[3]),
    ]
    for load in loads:
        load.start()

    barrier = pltpu.get_barrier_semaphore()
    partners = [by_x, by_y, by_c] + [place(y, planes[step], x, c) for step in range(1, Z)]
    for partner in partners:
        pl.semaphore_signal(barrier, inc=1, device_id=partner, device_id_type=MESH)

    slots = gate_ref.shape[0]
    names = lax.broadcasted_iota(jnp.int32, (LANES, rows), 0)
    weights = jnp.zeros((LANES, rows), jnp.float32)
    for k in range(slots):
        gate, chosen = gate_ref[k : k + 1, :], ids_ref[k : k + 1, :]
        high = gate.astype(jnp.bfloat16).astype(jnp.float32)
        weights += jnp.where(names == chosen, high, 0.0)
        weights += jnp.where(names == chosen + experts, gate - high, 0.0)
    square = (rows, rows)
    diagonal = lax.broadcasted_iota(jnp.int32, square, 0) == lax.broadcasted_iota(jnp.int32, square, 1)
    turned = lax.dot_general(
        jnp.where(diagonal, 1.0, 0.0).astype(jnp.bfloat16), weights.astype(jnp.bfloat16),
        (((1,), (1,)), ((), ())), preferred_element_type=jnp.float32,
    )
    gathered[0, c, y, x, :, :LANES] = turned.astype(jnp.bfloat16)
    loads[0].wait()
    loads[1].wait()
    pl.semaphore_wait(barrier, len(partners))

    started = []

    def prepare(src, dst, device):
        index = len(started)
        copy = pltpu.make_async_remote_copy(
            src_ref=src, dst_ref=dst, send_sem=send_sem.at[index], recv_sem=recv_sem.at[index],
            device_id=device, device_id_type=MESH,
        )
        started.append(copy)
        return copy

    def send(src, dst, device):
        copy = prepare(src, dst, device)
        copy.start()
        return copy

    first_cols, second_cols = pl.ds(0, near), pl.ds(near, width)
    pending = {}

    for j in range(1, Z):
        pending["z", j] = prepare(
            gathered.at[0, c, y, x], gathered.at[j, c, y, x], place(y, planes[j], x, c)
        )

    def send_plane(j):
        pending["z", j].start()

    def send_inner(j):
        @pl.when(inner)
        def _():
            pending["z", j].start()

    def send_outer(j):
        @pl.when(jnp.logical_not(inner))
        def _():
            pending["z", j].start()

    def gather_first(j):
        if j:
            pending["z", j].wait_recv()
        for name, cols, device in (("fa", first_cols, by_x), ("fb", second_cols, by_y)):
            ref = gathered.at[j, c, y, x, :, cols]
            pending[name, j] = send(ref, ref, device)

    def gather_second(j):
        pending["fa", j].wait_recv()
        ref = gathered.at[j, c, y, :, :, first_cols]
        pending["sa", j] = send(ref, ref, by_y)
        pending["fb", j].wait_recv()
        ref = gathered.at[j, c, :, x, :, second_cols]
        pending["sb", j] = send(ref, ref, by_x)

    def gather_core(j):
        pending["sa", j].wait_recv()
        pending["sb", j].wait_recv()
        ref = gathered.at[j, c]
        pending["c", j] = send(ref, ref, by_c)

    def evaluate(j):
        pending["c", j].wait_recv()
        if j == 0:
            loads[2].wait()
            loads[3].wait()
        group = C * Y * X * rows
        features = gathered[j, :, :, :, :, LANES:near].reshape(group, width)
        row_grads = gathered[j, :, :, :, :, near:].reshape(group, width)
        extra = gathered[j, :, :, :, :, :LANES].reshape(group, LANES).astype(jnp.float32)
        lanes = lax.broadcasted_iota(jnp.int32, (group, LANES), 1)
        mine = lanes == expert
        weight = jnp.sum(jnp.where(mine | (lanes == expert + experts), extra, 0.0), 1, keepdims=True)
        contract = (((1,), (1,)), ((), ()))
        pre_act = lax.dot_general(features, up[...], contract, preferred_element_type=jnp.float32)
        gating = jax.nn.sigmoid(pre_act)
        hidden = (pre_act * gating).astype(jnp.bfloat16)
        hidden_grad = lax.dot_general(row_grads, down[...], contract, preferred_element_type=jnp.float32)
        act_grad = (hidden_grad * gating * (1.0 + pre_act * (1.0 - gating))).astype(jnp.bfloat16)
        products = jnp.sum(hidden.astype(jnp.float32) * hidden_grad, 1, keepdims=True)
        partial[j, :, :, :, :, :LANES] = (
            jnp.where(mine, products, 0.0).astype(jnp.bfloat16).reshape(C, Y, X, rows, LANES)
        )
        tile = min(512, width)
        for left, matrix, base in ((hidden, down, LANES), (act_grad, up, near)):
            for at in range(0, width, tile):
                result = jnp.dot(left, matrix[:, at : at + tile], preferred_element_type=jnp.float32)
                partial[j, :, :, :, :, base + at : base + at + tile] = (
                    (result * weight).astype(jnp.bfloat16).reshape(C, Y, X, rows, tile)
                )
        pending["rc", j] = send(partial.at[j, far_c], from_core.at[j], by_c)

    def add(one, other):
        return (one.astype(jnp.float32) + other.astype(jnp.float32)).astype(jnp.bfloat16)

    def reduce_first(j):
        pending["rc", j].wait_recv()
        core_sum[j] = add(partial[j, c], from_core[j])
        pending["ra", j] = send(
            core_sum.at[j, far_y, :, :, first_cols], from_first.at[j, :, :, first_cols], by_y
        )
        pending["rb", j] = send(
            core_sum.at[j, :, far_x, :, second_cols], from_first.at[j, :, :, second_cols], by_x
        )

    def reduce_second(j):
        pending["ra", j].wait_recv()
        first_sum[j, :, :, :near] = add(core_sum[j, y, :, :, :near], from_first[j, :, :, :near])
        pending["sra", j] = send(
            first_sum.at[j, far_x, :, first_cols], from_second.at[j, :, first_cols], by_x
        )
        pending["rb", j].wait_recv()
        for yy in range(Y):
            first_sum[j, yy, :, near:] = add(core_sum[j, yy, x, :, near:], from_first[j, yy, :, near:])
        pending["srb", j] = send(
            first_sum.at[j, far_y, :, second_cols], from_second.at[j, :, second_cols], by_y
        )

    def reduce_plane(j):
        pending["sra", j].wait_recv()
        pending["srb", j].wait_recv()
        plane_sum[j, :, :near] = add(first_sum[j, x, :, :near], from_second[j, :, :near])
        plane_sum[j, :, near:] = add(first_sum[j, y, :, near:], from_second[j, :, near:])
        if j:
            pending["rz", j] = send(plane_sum.at[j], from_z.at[j], place(y, planes[j], x, c))

    order = (
        (send_plane, 1), (send_inner, 2), (gather_first, 0), (gather_second, 0), (send_outer, 2),
        (gather_first, 1), (send_plane, 3), (gather_core, 0), (gather_first, 2), (gather_second, 1),
        (evaluate, 0), (gather_second, 2), (gather_core, 1), (gather_first, 3), (evaluate, 1),
        (gather_core, 2), (gather_second, 3), (reduce_first, 1), (evaluate, 2),
        (gather_core, 3), (reduce_first, 2), (evaluate, 3), (reduce_second, 1),
        (reduce_first, 3), (reduce_second, 2), (reduce_plane, 1), (reduce_second, 3), (reduce_first, 0),
        (reduce_plane, 2), (reduce_plane, 3), (reduce_second, 0), (reduce_plane, 0),
    )
    for stage, j in order:
        stage(j)

    total = plane_sum[0].astype(jnp.float32)
    for j in range(1, Z):
        pending["rz", j].wait_recv()
        total += from_z[j].astype(jnp.float32)
    mixture_ref[...] = total[:, LANES:near].astype(jnp.bfloat16)
    input_grad_ref[...] = total[:, near:].astype(jnp.bfloat16)
    per_expert = lax.dot_general(
        total[:, :LANES], jnp.where(diagonal, 1.0, 0.0), (((0,), (0,)), ((), ())),
        precision=lax.Precision.HIGHEST, preferred_element_type=jnp.float32,
    )
    for k in range(slots):
        gate_grad_ref[k : k + 1, :] = jnp.sum(
            jnp.where(names == ids_ref[k : k + 1, :], per_expert, 0.0), 0, keepdims=True
        )
    for copy in started:
        copy.wait_send()


def token_shards(tokens, cotangent, gate_probs, expert_ids, up_weight, down_weight):
    rows, width = tokens.shape
    experts = lax.axis_size("expert")
    hidden_part = up_weight.shape[1]
    wide = LANES + 2 * width
    kind = jnp.bfloat16
    copies = 2 * (Z - 1) + 11 * Z
    vmem = pl.BlockSpec(memory_space=pltpu.VMEM)
    hbm = pl.BlockSpec(memory_space=pl.ANY)
    mixture, input_grad, gate_grad = pl.pallas_call(
        functools.partial(exchange_kernel, experts),
        out_shape=(
            jax.ShapeDtypeStruct((rows, width), kind),
            jax.ShapeDtypeStruct((rows, width), kind),
            jax.ShapeDtypeStruct(gate_probs.shape[::-1], jnp.float32),
        ),
        in_specs=[hbm, hbm, vmem, vmem, hbm, hbm],
        out_specs=(vmem, vmem, vmem),
        scratch_shapes=[
            pltpu.VMEM((hidden_part, width), kind),
            pltpu.VMEM((hidden_part, width), kind),
            pltpu.VMEM((Z, C, Y, X, rows, wide), kind),
            pltpu.VMEM((Z, C, Y, X, rows, wide), kind),
            pltpu.VMEM((Z, Y, X, rows, wide), kind),
            pltpu.VMEM((Z, Y, X, rows, wide), kind),
            pltpu.VMEM((Z, 2, rows, wide), kind),
            pltpu.VMEM((Z, 2, rows, wide), kind),
            pltpu.VMEM((Z, rows, wide), kind),
            pltpu.VMEM((Z, rows, wide), kind),
            pltpu.VMEM((Z, rows, wide), kind),
            pltpu.SemaphoreType.DMA((4,)),
            pltpu.SemaphoreType.DMA((copies,)),
            pltpu.SemaphoreType.DMA((copies,)),
        ],
        compiler_params=pltpu.CompilerParams(
            collective_id=0, has_side_effects=True, vmem_limit_bytes=60 * 1024 * 1024
        ),
    )(tokens, cotangent, gate_probs.T, expert_ids.T, up_weight, down_weight)
    return mixture, input_grad, gate_grad.T


def solution(mesh):
    small = dict(mesh.shape) == {"dp": Y, "expert": Z * X * C}
    placed = (
        P(("dp", "expert"), None),
        P(("dp", "expert"), None),
        P(("dp", "expert"), None),
        P(("dp", "expert"), None),
        P("expert", "dp", None),
        P("expert", "dp", None),
    )
    return jax.shard_map(
        token_shards if small else shards,
        mesh=mesh,
        in_specs=placed,
        out_specs=(P(("dp", "expert"), None), P(("dp", "expert"), None), P(("dp", "expert"), None)),
        check_vma=False,
    )
```

```python
import functools

import jax
import jax.numpy as jnp
from jax import lax
from jax.experimental import pallas as pl
from jax.experimental.pallas import tpu as pltpu
from jax.sharding import PartitionSpec as P


def broadcast(block, axis, owner):
    block = jnp.where(lax.axis_index(axis) == owner, block, jnp.zeros_like(block))
    return lax.psum(block, axis)


def expert_terms(row_block, up_piece, down_piece):
    model_width = row_block.shape[1] // 2
    features = row_block[:, :model_width]
    row_grads = row_block[:, model_width:]
    pre_act = jnp.einsum("rd,hd->rh", features, up_piece, preferred_element_type=jnp.float32)
    gating = jax.nn.sigmoid(pre_act)
    hidden = (pre_act * gating).astype(jnp.bfloat16)
    output_rows = jnp.dot(hidden, down_piece, preferred_element_type=jnp.float32)
    hidden_grad = jnp.einsum("rd,hd->rh", row_grads, down_piece, preferred_element_type=jnp.float32)
    act_grad = (hidden_grad * gating * (1.0 + pre_act * (1.0 - gating))).astype(jnp.bfloat16)
    input_rows = jnp.dot(act_grad, up_piece, preferred_element_type=jnp.float32)
    return jnp.concatenate([output_rows, input_rows], 1)


def spread(up_parts, down_parts, row_sets):
    model_width = up_parts.shape[2]
    initial = tuple(
        (jnp.zeros((row_block.shape[0], 2 * model_width), jnp.float32) for row_block in row_sets)
    )
    up_piece = lax.all_gather(up_parts, "dp", axis=1, tiled=True)
    down_piece = lax.all_gather(down_parts, "dp", axis=1, tiled=True)
    return tuple(
        (
            expert_terms(row_block, up_piece[member], down_piece[member])
            for member, (running, row_block) in enumerate(zip(initial, row_sets))
        )
    )


def shards(tokens, cotangent, gate_probs, expert_ids, up_weight, down_weight):
    tok_rows, model_width = tokens.shape
    top_count = expert_ids.shape[1]
    experts = lax.axis_size("expert")
    hot_rows = 9 * tok_rows // 16
    cold_total = experts - 1
    capacity = (tok_rows * top_count - hot_rows + cold_total - 1) // cold_total
    flat_ids = expert_ids.reshape(-1)
    slot_count = flat_ids.shape[0]
    one_hot = (flat_ids[:, None] == jnp.arange(experts, dtype=jnp.int32)[None, :]).astype(jnp.int32)
    hottest = jnp.argmax(jnp.sum(one_hot, 0))
    before = jnp.cumsum(one_hot, 0) - one_hot
    slot_rank = jnp.sum(before * one_hot, 1)
    slot_total = experts * capacity + hot_rows
    slot_index = jnp.where(
        flat_ids == hottest, experts * capacity + slot_rank, flat_ids * capacity + slot_rank
    )
    source_slot = (
        jnp.full((slot_total,), slot_count, jnp.int32)
        .at[slot_index]
        .set(jnp.arange(slot_count, dtype=jnp.int32))
    )
    source_row = source_slot // top_count
    payload = jnp.concatenate([tokens, cotangent], 1)
    padded_payload = jnp.concatenate([payload, jnp.zeros((1, 2 * model_width), payload.dtype)], 0)
    placed = padded_payload[source_row]
    outgoing = placed[: experts * capacity].reshape(experts, capacity, 2 * model_width)
    local_rows = placed[experts * capacity :]
    arrived = lax.all_to_all(outgoing, "expert", split_axis=0, concat_axis=0, tiled=True)
    arrived_rows = arrived.reshape(experts * capacity, 2 * model_width)
    shadow_up, shadow_down = (
        broadcast(up_weight[0], "expert", hottest),
        broadcast(down_weight[0], "expert", hottest),
    )
    (own_out,) = spread(up_weight, down_weight, [arrived_rows])
    (hot_out,) = spread(shadow_up[None], shadow_down[None], [local_rows])
    returning = own_out.astype(jnp.bfloat16).reshape(experts, capacity, 2 * model_width)
    came_back = lax.all_to_all(returning, "expert", split_axis=0, concat_axis=0, tiled=True)
    results = jnp.concatenate(
        [came_back.reshape(experts * capacity, 2 * model_width), hot_out.astype(jnp.bfloat16)], 0
    )
    per_slot = results[slot_index].astype(jnp.float32).reshape(tok_rows, top_count, 2 * model_width)
    scale = gate_probs[:, :, None]
    mixture = jnp.sum(scale * per_slot[:, :, :model_width], 1).astype(jnp.bfloat16)
    input_grad = jnp.sum(scale * per_slot[:, :, model_width:], 1).astype(jnp.bfloat16)
    gate_grad = jnp.sum(cotangent.astype(jnp.float32)[:, None, :] * per_slot[:, :, :model_width], 2)
    return (mixture, input_grad, gate_grad)


MESH = pl.DeviceIdType.MESH
LANES = 128
Z, Y, X, C = 4, 2, 2, 2


def exchange_kernel(
    experts,
    tokens_hbm, cotangent_hbm, gate_ref, ids_ref, up_hbm, down_hbm,
    mixture_ref, input_grad_ref, gate_grad_ref,
    up, down, up_turned, down_turned, gathered, partial, from_core, core_sum, from_first, first_sum, from_second, plane_sum, from_z,
    load_sem, send_sem, recv_sem,
):
    width = tokens_hbm.shape[1]
    near = LANES + width
    rows = tokens_hbm.shape[0]
    y, expert = lax.axis_index("dp"), lax.axis_index("expert")
    z = expert // (X * C)
    x = (expert // C) % X
    c = expert % C
    far_y, far_x, far_c = 1 - y, 1 - x, 1 - c

    def place(yy, zz, xx, cc):
        return (yy, (zz * X + xx) * C + cc)

    by_x, by_y, by_c = place(y, z, far_x, c), place(far_y, z, x, c), place(y, z, x, far_c)
    planes = [z, z + 1 - 2 * (z % 2), Z - 1 - z, (z + 2) % Z]
    inner = z % (Z - 1) > 0

    loads = [
        pltpu.make_async_copy(tokens_hbm, gathered.at[0, c, y, x, :, pl.ds(LANES, width)], load_sem.at[0]),
        pltpu.make_async_copy(cotangent_hbm, gathered.at[0, c, y, x, :, pl.ds(near, width)], load_sem.at[1]),
        pltpu.make_async_copy(up_hbm.at[0], up, load_sem.at[2]),
        pltpu.make_async_copy(down_hbm.at[0], down, load_sem.at[3]),
    ]
    for load in loads:
        load.start()

    barrier = pltpu.get_barrier_semaphore()
    partners = [by_x, by_y, by_c] + [place(y, planes[step], x, c) for step in range(1, Z)]
    for partner in partners:
        pl.semaphore_signal(barrier, inc=1, device_id=partner, device_id_type=MESH)

    slots = gate_ref.shape[0]
    names = lax.broadcasted_iota(jnp.int32, (LANES, rows), 0)
    weights = jnp.zeros((LANES, rows), jnp.float32)
    for k in range(slots):
        gate, chosen = gate_ref[k : k + 1, :], ids_ref[k : k + 1, :]
        high = gate.astype(jnp.bfloat16).astype(jnp.float32)
        weights += jnp.where(names == chosen, high, 0.0)
        weights += jnp.where(names == chosen + experts, gate - high, 0.0)
    square = (rows, rows)
    diagonal = lax.broadcasted_iota(jnp.int32, square, 0) == lax.broadcasted_iota(jnp.int32, square, 1)
    turned = lax.dot_general(
        jnp.where(diagonal, 1.0, 0.0).astype(jnp.bfloat16), weights.astype(jnp.bfloat16),
        (((1,), (1,)), ((), ())), preferred_element_type=jnp.float32,
    )
    gathered[0, c, y, x, :, :LANES] = turned.astype(jnp.bfloat16)
    loads[0].wait()
    loads[1].wait()
    pl.semaphore_wait(barrier, len(partners))

    started = []

    def prepare(src, dst, device):
        index = len(started)
        copy = pltpu.make_async_remote_copy(
            src_ref=src, dst_ref=dst, send_sem=send_sem.at[index], recv_sem=recv_sem.at[index],
            device_id=device, device_id_type=MESH,
        )
        started.append(copy)
        return copy

    def send(src, dst, device):
        copy = prepare(src, dst, device)
        copy.start()
        return copy

    first_cols, second_cols = pl.ds(0, near), pl.ds(near, width)
    pending = {}

    for j in range(1, Z):
        pending["z", j] = prepare(
            gathered.at[0, c, y, x], gathered.at[j, c, y, x], place(y, planes[j], x, c)
        )

    def send_plane(j):
        pending["z", j].start()

    def send_inner(j):
        @pl.when(inner)
        def _():
            pending["z", j].start()

    def send_outer(j):
        @pl.when(jnp.logical_not(inner))
        def _():
            pending["z", j].start()

    def gather_first(j):
        if j:
            pending["z", j].wait_recv()
        for name, cols, device in (("fa", first_cols, by_x), ("fb", second_cols, by_y)):
            ref = gathered.at[j, c, y, x, :, cols]
            pending[name, j] = send(ref, ref, device)

    def gather_second(j):
        pending["fa", j].wait_recv()
        ref = gathered.at[j, c, y, :, :, first_cols]
        pending["sa", j] = send(ref, ref, by_y)
        pending["fb", j].wait_recv()
        ref = gathered.at[j, c, :, x, :, second_cols]
        pending["sb", j] = send(ref, ref, by_x)

    def gather_core(j):
        pending["sa", j].wait_recv()
        pending["sb", j].wait_recv()
        ref = gathered.at[j, c]
        pending["c", j] = send(ref, ref, by_c)

    def turn(index):
        loads[2 + index].wait()
        matrix, turned = ((up, up_turned), (down, down_turned))[index]
        block = min(256, width)
        for at in range(0, width, block):
            turned[at : at + block, :] = matrix[:, at : at + block].T

    def evaluate(j):
        pending["c", j].wait_recv()
        group = C * Y * X * rows
        features = gathered[j, :, :, :, :, LANES:near].reshape(group, width)
        row_grads = gathered[j, :, :, :, :, near:].reshape(group, width)
        extra = gathered[j, :, :, :, :, :LANES].reshape(group, LANES).astype(jnp.float32)
        lanes = lax.broadcasted_iota(jnp.int32, (group, LANES), 1)
        mine = lanes == expert
        weight = jnp.sum(jnp.where(mine | (lanes == expert + experts), extra, 0.0), 1, keepdims=True)
        pre_act = jnp.dot(features, up_turned[...], preferred_element_type=jnp.float32)
        gating = jax.nn.sigmoid(pre_act)
        hidden = (pre_act * gating).astype(jnp.bfloat16)
        hidden_grad = jnp.dot(row_grads, down_turned[...], preferred_element_type=jnp.float32)
        act_grad = (hidden_grad * gating * (1.0 + pre_act * (1.0 - gating))).astype(jnp.bfloat16)
        products = jnp.sum(hidden.astype(jnp.float32) * hidden_grad, 1, keepdims=True)
        partial[j, :, :, :, :, :LANES] = (
            jnp.where(mine, products, 0.0).astype(jnp.bfloat16).reshape(C, Y, X, rows, LANES)
        )
        tile = min(512, width)
        for left, matrix, base in ((hidden, down, LANES), (act_grad, up, near)):
            for at in range(0, width, tile):
                result = jnp.dot(left, matrix[:, at : at + tile], preferred_element_type=jnp.float32)
                partial[j, :, :, :, :, base + at : base + at + tile] = (
                    (result * weight).astype(jnp.bfloat16).reshape(C, Y, X, rows, tile)
                )
        pending["rc", j] = send(partial.at[j, far_c], from_core.at[j], by_c)

    def add(one, other):
        return (one.astype(jnp.float32) + other.astype(jnp.float32)).astype(jnp.bfloat16)

    def reduce_first(j):
        pending["rc", j].wait_recv()
        core_sum[j] = add(partial[j, c], from_core[j])
        pending["ra", j] = send(
            core_sum.at[j, far_y, :, :, first_cols], from_first.at[j, :, :, first_cols], by_y
        )
        pending["rb", j] = send(
            core_sum.at[j, :, far_x, :, second_cols], from_first.at[j, :, :, second_cols], by_x
        )

    def reduce_second(j):
        pending["ra", j].wait_recv()
        first_sum[j, :, :, :near] = add(core_sum[j, y, :, :, :near], from_first[j, :, :, :near])
        pending["sra", j] = send(
            first_sum.at[j, far_x, :, first_cols], from_second.at[j, :, first_cols], by_x
        )
        pending["rb", j].wait_recv()
        for yy in range(Y):
            first_sum[j, yy, :, near:] = add(core_sum[j, yy, x, :, near:], from_first[j, yy, :, near:])
        pending["srb", j] = send(
            first_sum.at[j, far_y, :, second_cols], from_second.at[j, :, second_cols], by_y
        )

    def reduce_plane(j):
        pending["sra", j].wait_recv()
        pending["srb", j].wait_recv()
        plane_sum[j, :, :near] = add(first_sum[j, x, :, :near], from_second[j, :, :near])
        plane_sum[j, :, near:] = add(first_sum[j, y, :, near:], from_second[j, :, near:])
        if j:
            pending["rz", j] = send(plane_sum.at[j], from_z.at[j], place(y, planes[j], x, c))

    order = (
        (send_plane, 1), (send_inner, 2), (gather_first, 0), (turn, 0), (gather_second, 0), (send_outer, 2),
        (turn, 1),
        (gather_first, 1), (send_plane, 3), (gather_core, 0), (gather_first, 2), (gather_second, 1),
        (evaluate, 0), (gather_second, 2), (gather_core, 1), (gather_first, 3), (evaluate, 1),
        (gather_core, 2), (gather_second, 3), (reduce_first, 1), (evaluate, 2),
        (gather_core, 3), (reduce_first, 2), (evaluate, 3), (reduce_second, 1),
        (reduce_first, 3), (reduce_second, 2), (reduce_plane, 1), (reduce_second, 3), (reduce_first, 0),
        (reduce_plane, 2), (reduce_plane, 3), (reduce_second, 0), (reduce_plane, 0),
    )
    for stage, j in order:
        stage(j)

    total = plane_sum[0].astype(jnp.float32)
    for j in range(1, Z):
        pending["rz", j].wait_recv()
        total += from_z[j].astype(jnp.float32)
    mixture_ref[...] = total[:, LANES:near].astype(jnp.bfloat16)
    input_grad_ref[...] = total[:, near:].astype(jnp.bfloat16)
    per_expert = lax.dot_general(
        total[:, :LANES], jnp.where(diagonal, 1.0, 0.0), (((0,), (0,)), ((), ())),
        precision=lax.Precision.HIGHEST, preferred_element_type=jnp.float32,
    )
    for k in range(slots):
        gate_grad_ref[k : k + 1, :] = jnp.sum(
            jnp.where(names == ids_ref[k : k + 1, :], per_expert, 0.0), 0, keepdims=True
        )
    for copy in started:
        copy.wait_send()


def token_shards(tokens, cotangent, gate_probs, expert_ids, up_weight, down_weight):
    rows, width = tokens.shape
    experts = lax.axis_size("expert")
    hidden_part = up_weight.shape[1]
    wide = LANES + 2 * width
    kind = jnp.bfloat16
    copies = 2 * (Z - 1) + 11 * Z
    vmem = pl.BlockSpec(memory_space=pltpu.VMEM)
    hbm = pl.BlockSpec(memory_space=pl.ANY)
    mixture, input_grad, gate_grad = pl.pallas_call(
        functools.partial(exchange_kernel, experts),
        out_shape=(
            jax.ShapeDtypeStruct((rows, width), kind),
            jax.ShapeDtypeStruct((rows, width), kind),
            jax.ShapeDtypeStruct(gate_probs.shape[::-1], jnp.float32),
        ),
        in_specs=[hbm, hbm, vmem, vmem, hbm, hbm],
        out_specs=(vmem, vmem, vmem),
        scratch_shapes=[
            pltpu.VMEM((hidden_part, width), kind),
            pltpu.VMEM((hidden_part, width), kind),
            pltpu.VMEM((width, hidden_part), kind),
            pltpu.VMEM((width, hidden_part), kind),
            pltpu.VMEM((Z, C, Y, X, rows, wide), kind),
            pltpu.VMEM((Z, C, Y, X, rows, wide), kind),
            pltpu.VMEM((Z, Y, X, rows, wide), kind),
            pltpu.VMEM((Z, Y, X, rows, wide), kind),
            pltpu.VMEM((Z, 2, rows, wide), kind),
            pltpu.VMEM((Z, 2, rows, wide), kind),
            pltpu.VMEM((Z, rows, wide), kind),
            pltpu.VMEM((Z, rows, wide), kind),
            pltpu.VMEM((Z, rows, wide), kind),
            pltpu.SemaphoreType.DMA((4,)),
            pltpu.SemaphoreType.DMA((copies,)),
            pltpu.SemaphoreType.DMA((copies,)),
        ],
        compiler_params=pltpu.CompilerParams(
            collective_id=0, has_side_effects=True, vmem_limit_bytes=53500 * 1024
        ),
    )(tokens, cotangent, gate_probs.T, expert_ids.T, up_weight, down_weight)
    return mixture, input_grad, gate_grad.T


def solution(mesh):
    small = dict(mesh.shape) == {"dp": Y, "expert": Z * X * C}
    placed = (
        P(("dp", "expert"), None),
        P(("dp", "expert"), None),
        P(("dp", "expert"), None),
        P(("dp", "expert"), None),
        P("expert", "dp", None),
        P("expert", "dp", None),
    )
    return jax.shard_map(
        token_shards if small else shards,
        mesh=mesh,
        in_specs=placed,
        out_specs=(P(("dp", "expert"), None), P(("dp", "expert"), None), P(("dp", "expert"), None)),
        check_vma=False,
    )
```

```python
import functools

import jax
import jax.numpy as jnp
from jax import lax
from jax.experimental import pallas as pl
from jax.experimental.pallas import tpu as pltpu
from jax.sharding import PartitionSpec as P


def broadcast(block, axis, owner):
    block = jnp.where(lax.axis_index(axis) == owner, block, jnp.zeros_like(block))
    return lax.psum(block, axis)


def expert_terms(row_block, up_piece, down_piece):
    model_width = row_block.shape[1] // 2
    features = row_block[:, :model_width]
    row_grads = row_block[:, model_width:]
    pre_act = jnp.einsum("rd,hd->rh", features, up_piece, preferred_element_type=jnp.float32)
    gating = jax.nn.sigmoid(pre_act)
    hidden = (pre_act * gating).astype(jnp.bfloat16)
    output_rows = jnp.dot(hidden, down_piece, preferred_element_type=jnp.float32)
    hidden_grad = jnp.einsum("rd,hd->rh", row_grads, down_piece, preferred_element_type=jnp.float32)
    act_grad = (hidden_grad * gating * (1.0 + pre_act * (1.0 - gating))).astype(jnp.bfloat16)
    input_rows = jnp.dot(act_grad, up_piece, preferred_element_type=jnp.float32)
    return jnp.concatenate([output_rows, input_rows], 1)


def spread(up_parts, down_parts, row_sets):
    model_width = up_parts.shape[2]
    initial = tuple(
        (jnp.zeros((row_block.shape[0], 2 * model_width), jnp.float32) for row_block in row_sets)
    )
    up_piece = lax.all_gather(up_parts, "dp", axis=1, tiled=True)
    down_piece = lax.all_gather(down_parts, "dp", axis=1, tiled=True)
    return tuple(
        (
            expert_terms(row_block, up_piece[member], down_piece[member])
            for member, (running, row_block) in enumerate(zip(initial, row_sets))
        )
    )


def shards(tokens, cotangent, gate_probs, expert_ids, up_weight, down_weight):
    tok_rows, model_width = tokens.shape
    top_count = expert_ids.shape[1]
    experts = lax.axis_size("expert")
    hot_rows = 9 * tok_rows // 16
    cold_total = experts - 1
    capacity = (tok_rows * top_count - hot_rows + cold_total - 1) // cold_total
    flat_ids = expert_ids.reshape(-1)
    slot_count = flat_ids.shape[0]
    one_hot = (flat_ids[:, None] == jnp.arange(experts, dtype=jnp.int32)[None, :]).astype(jnp.int32)
    hottest = jnp.argmax(jnp.sum(one_hot, 0))
    before = jnp.cumsum(one_hot, 0) - one_hot
    slot_rank = jnp.sum(before * one_hot, 1)
    slot_total = experts * capacity + hot_rows
    slot_index = jnp.where(
        flat_ids == hottest, experts * capacity + slot_rank, flat_ids * capacity + slot_rank
    )
    source_slot = (
        jnp.full((slot_total,), slot_count, jnp.int32)
        .at[slot_index]
        .set(jnp.arange(slot_count, dtype=jnp.int32))
    )
    source_row = source_slot // top_count
    payload = jnp.concatenate([tokens, cotangent], 1)
    padded_payload = jnp.concatenate([payload, jnp.zeros((1, 2 * model_width), payload.dtype)], 0)
    placed = padded_payload[source_row]
    outgoing = placed[: experts * capacity].reshape(experts, capacity, 2 * model_width)
    local_rows = placed[experts * capacity :]
    arrived = lax.all_to_all(outgoing, "expert", split_axis=0, concat_axis=0, tiled=True)
    arrived_rows = arrived.reshape(experts * capacity, 2 * model_width)
    shadow_up, shadow_down = (
        broadcast(up_weight[0], "expert", hottest),
        broadcast(down_weight[0], "expert", hottest),
    )
    (own_out,) = spread(up_weight, down_weight, [arrived_rows])
    (hot_out,) = spread(shadow_up[None], shadow_down[None], [local_rows])
    returning = own_out.astype(jnp.bfloat16).reshape(experts, capacity, 2 * model_width)
    came_back = lax.all_to_all(returning, "expert", split_axis=0, concat_axis=0, tiled=True)
    results = jnp.concatenate(
        [came_back.reshape(experts * capacity, 2 * model_width), hot_out.astype(jnp.bfloat16)], 0
    )
    per_slot = results[slot_index].astype(jnp.float32).reshape(tok_rows, top_count, 2 * model_width)
    scale = gate_probs[:, :, None]
    mixture = jnp.sum(scale * per_slot[:, :, :model_width], 1).astype(jnp.bfloat16)
    input_grad = jnp.sum(scale * per_slot[:, :, model_width:], 1).astype(jnp.bfloat16)
    gate_grad = jnp.sum(cotangent.astype(jnp.float32)[:, None, :] * per_slot[:, :, :model_width], 2)
    return (mixture, input_grad, gate_grad)


MESH = pl.DeviceIdType.MESH
LANES = 128
Z, Y, X, C = 4, 2, 2, 2


def exchange_kernel(
    experts,
    tokens_hbm, cotangent_hbm, gate_ref, ids_ref, up_hbm, down_hbm,
    mixture_ref, input_grad_ref, gate_grad_ref,
    up, down, up_turned, down_turned, gathered, partial, from_core, core_sum, from_first, first_sum, from_second, plane_sum, from_z,
    load_sem, send_sem, recv_sem,
):
    width = tokens_hbm.shape[1]
    near = LANES + width
    rows = tokens_hbm.shape[0]
    y, expert = lax.axis_index("dp"), lax.axis_index("expert")
    z = expert // (X * C)
    x = (expert // C) % X
    c = expert % C
    far_y, far_x, far_c = 1 - y, 1 - x, 1 - c

    def place(yy, zz, xx, cc):
        return (yy, (zz * X + xx) * C + cc)

    by_x, by_y, by_c = place(y, z, far_x, c), place(far_y, z, x, c), place(y, z, x, far_c)
    planes = [z, z + 1 - 2 * (z % 2), Z - 1 - z, (z + 2) % Z]
    inner = z % (Z - 1) > 0

    loads = [
        pltpu.make_async_copy(tokens_hbm, gathered.at[0, c, y, x, :, pl.ds(LANES, width)], load_sem.at[0]),
        pltpu.make_async_copy(cotangent_hbm, gathered.at[0, c, y, x, :, pl.ds(near, width)], load_sem.at[1]),
        pltpu.make_async_copy(up_hbm.at[0], up, load_sem.at[2]),
        pltpu.make_async_copy(down_hbm.at[0], down, load_sem.at[3]),
    ]
    for load in loads:
        load.start()

    barrier = pltpu.get_barrier_semaphore()
    partners = [by_x, by_y, by_c] + [place(y, planes[step], x, c) for step in range(1, Z)]
    for partner in partners:
        pl.semaphore_signal(barrier, inc=1, device_id=partner, device_id_type=MESH)

    slots = gate_ref.shape[0]
    names = lax.broadcasted_iota(jnp.int32, (LANES, rows), 0)
    weights = jnp.zeros((LANES, rows), jnp.float32)
    for k in range(slots):
        gate, chosen = gate_ref[k : k + 1, :], ids_ref[k : k + 1, :]
        high = gate.astype(jnp.bfloat16).astype(jnp.float32)
        weights += jnp.where(names == chosen, high, 0.0)
        weights += jnp.where(names == chosen + experts, gate - high, 0.0)
    square = (rows, rows)
    diagonal = lax.broadcasted_iota(jnp.int32, square, 0) == lax.broadcasted_iota(jnp.int32, square, 1)
    turned = lax.dot_general(
        jnp.where(diagonal, 1.0, 0.0).astype(jnp.bfloat16), weights.astype(jnp.bfloat16),
        (((1,), (1,)), ((), ())), preferred_element_type=jnp.float32,
    )
    gathered[0, c, y, x, :, :LANES] = turned.astype(jnp.bfloat16)
    loads[0].wait()
    loads[1].wait()
    pl.semaphore_wait(barrier, len(partners))

    started = []

    def prepare(src, dst, device):
        index = len(started)
        copy = pltpu.make_async_remote_copy(
            src_ref=src, dst_ref=dst, send_sem=send_sem.at[index], recv_sem=recv_sem.at[index],
            device_id=device, device_id_type=MESH,
        )
        started.append(copy)
        return copy

    def send(src, dst, device):
        copy = prepare(src, dst, device)
        copy.start()
        return copy

    first_cols, second_cols = pl.ds(0, near), pl.ds(near, width)
    pending = {}

    for j in range(1, Z):
        pending["z", j] = prepare(
            gathered.at[0, c, y, x], gathered.at[j, c, y, x], place(y, planes[j], x, c)
        )

    def send_plane(j):
        pending["z", j].start()

    def send_inner(j):
        @pl.when(inner)
        def _():
            pending["z", j].start()

    def send_outer(j):
        @pl.when(jnp.logical_not(inner))
        def _():
            pending["z", j].start()

    def gather_first(j):
        if j:
            pending["z", j].wait_recv()
        for name, cols, device in (("fa", first_cols, by_x), ("fb", second_cols, by_y)):
            ref = gathered.at[j, c, y, x, :, cols]
            pending[name, j] = send(ref, ref, device)

    def gather_second(j):
        pending["fa", j].wait_recv()
        ref = gathered.at[j, c, y, :, :, first_cols]
        pending["sa", j] = send(ref, ref, by_y)
        pending["fb", j].wait_recv()
        ref = gathered.at[j, c, :, x, :, second_cols]
        pending["sb", j] = send(ref, ref, by_x)

    def gather_core(j):
        for name, cols in (("a", first_cols), ("b", second_cols)):
            pending["s" + name, j].wait_recv()
            ref = gathered.at[j, c, :, :, :, cols]
            pending["c" + name, j] = send(ref, ref, by_c)

    def turn(index):
        loads[2 + index].wait()
        matrix, turned = ((up, up_turned), (down, down_turned))[index]
        block = min(256, width)
        for at in range(0, width, block):
            turned[at : at + block, :] = matrix[:, at : at + block].T

    def evaluate(j):
        pending["ca", j].wait_recv()
        group = C * Y * X * rows
        features = gathered[j, :, :, :, :, LANES:near].reshape(group, width)
        extra = gathered[j, :, :, :, :, :LANES].reshape(group, LANES).astype(jnp.float32)
        lanes = lax.broadcasted_iota(jnp.int32, (group, LANES), 1)
        mine = lanes == expert
        weight = jnp.sum(jnp.where(mine | (lanes == expert + experts), extra, 0.0), 1, keepdims=True)
        pre_act = jnp.dot(features, up_turned[...], preferred_element_type=jnp.float32)
        gating = jax.nn.sigmoid(pre_act)
        hidden = (pre_act * gating).astype(jnp.bfloat16)
        pending["cb", j].wait_recv()
        row_grads = gathered[j, :, :, :, :, near:].reshape(group, width)
        hidden_grad = jnp.dot(row_grads, down_turned[...], preferred_element_type=jnp.float32)
        act_grad = (hidden_grad * gating * (1.0 + pre_act * (1.0 - gating))).astype(jnp.bfloat16)
        products = jnp.sum(hidden.astype(jnp.float32) * hidden_grad, 1, keepdims=True)
        partial[j, :, :, :, :, :LANES] = (
            jnp.where(mine, products, 0.0).astype(jnp.bfloat16).reshape(C, Y, X, rows, LANES)
        )
        tile = min(512, width)
        for name, left, matrix, base, cols in (
            ("rca", hidden, down, LANES, first_cols), ("rcb", act_grad, up, near, second_cols)
        ):
            for at in range(0, width, tile):
                result = jnp.dot(left, matrix[:, at : at + tile], preferred_element_type=jnp.float32)
                partial[j, :, :, :, :, base + at : base + at + tile] = (
                    (result * weight).astype(jnp.bfloat16).reshape(C, Y, X, rows, tile)
                )
            pending[name, j] = send(
                partial.at[j, far_c, :, :, :, cols], from_core.at[j, :, :, :, cols], by_c
            )

    def add(one, other):
        return (one.astype(jnp.float32) + other.astype(jnp.float32)).astype(jnp.bfloat16)

    def reduce_first(j):
        pending["rca", j].wait_recv()
        core_sum[j, :, :, :, :near] = add(partial[j, c, :, :, :, :near], from_core[j, :, :, :, :near])
        pending["ra", j] = send(
            core_sum.at[j, far_y, :, :, first_cols], from_first.at[j, :, :, first_cols], by_y
        )
        pending["rcb", j].wait_recv()
        core_sum[j, :, :, :, near:] = add(partial[j, c, :, :, :, near:], from_core[j, :, :, :, near:])
        pending["rb", j] = send(
            core_sum.at[j, :, far_x, :, second_cols], from_first.at[j, :, :, second_cols], by_x
        )

    def reduce_second(j):
        pending["ra", j].wait_recv()
        first_sum[j, :, :, :near] = add(core_sum[j, y, :, :, :near], from_first[j, :, :, :near])
        pending["sra", j] = send(
            first_sum.at[j, far_x, :, first_cols], from_second.at[j, :, first_cols], by_x
        )
        pending["rb", j].wait_recv()
        for yy in range(Y):
            first_sum[j, yy, :, near:] = add(core_sum[j, yy, x, :, near:], from_first[j, yy, :, near:])
        pending["srb", j] = send(
            first_sum.at[j, far_y, :, second_cols], from_second.at[j, :, second_cols], by_y
        )

    def reduce_plane(j):
        for name, cols, kept in (
            ("a", slice(0, near), x), ("b", slice(near, near + width), y)
        ):
            pending["sr" + name, j].wait_recv()
            plane_sum[j, :, cols] = add(first_sum[j, kept, :, cols], from_second[j, :, cols])
            if j:
                part = first_cols if name == "a" else second_cols
                pending["rz" + name, j] = send(
                    plane_sum.at[j, :, part], from_z.at[j, :, part], place(y, planes[j], x, c)
                )

    order = (
        (send_plane, 1), (send_inner, 2), (gather_first, 0), (turn, 0), (gather_second, 0), (send_outer, 2),
        (turn, 1),
        (gather_first, 1), (send_plane, 3), (gather_core, 0), (gather_first, 2), (gather_second, 1),
        (evaluate, 0), (gather_second, 2), (gather_core, 1), (gather_first, 3), (evaluate, 1),
        (gather_core, 2), (gather_second, 3), (reduce_first, 1), (evaluate, 2),
        (gather_core, 3), (reduce_first, 2), (evaluate, 3), (reduce_second, 1),
        (reduce_first, 3), (reduce_second, 2), (reduce_plane, 1), (reduce_second, 3), (reduce_first, 0),
        (reduce_plane, 2), (reduce_plane, 3), (reduce_second, 0), (reduce_plane, 0),
    )
    for stage, j in order:
        stage(j)

    total = plane_sum[0].astype(jnp.float32)
    for j in range(1, Z):
        pending["rza", j].wait_recv()
        pending["rzb", j].wait_recv()
        total += from_z[j].astype(jnp.float32)
    mixture_ref[...] = total[:, LANES:near].astype(jnp.bfloat16)
    input_grad_ref[...] = total[:, near:].astype(jnp.bfloat16)
    per_expert = lax.dot_general(
        total[:, :LANES], jnp.where(diagonal, 1.0, 0.0), (((0,), (0,)), ((), ())),
        precision=lax.Precision.HIGHEST, preferred_element_type=jnp.float32,
    )
    for k in range(slots):
        gate_grad_ref[k : k + 1, :] = jnp.sum(
            jnp.where(names == ids_ref[k : k + 1, :], per_expert, 0.0), 0, keepdims=True
        )
    for copy in started:
        copy.wait_send()


def deliver_kernel(*refs):
    sem = refs[-1]
    half = (len(refs) - 1) // 2
    copies = [pltpu.make_async_copy(refs[i], refs[half + i], sem.at[i]) for i in range(half)]
    for copy in copies:
        copy.start()
    for copy in copies:
        copy.wait()


def token_shards(tokens, cotangent, gate_probs, expert_ids, up_weight, down_weight):
    rows, width = tokens.shape
    experts = lax.axis_size("expert")
    hidden_part = up_weight.shape[1]
    wide = LANES + 2 * width
    kind = jnp.bfloat16
    copies = 15 * Z
    vmem = pl.BlockSpec(memory_space=pltpu.VMEM)
    hbm = pl.BlockSpec(memory_space=pl.ANY)
    results = pl.pallas_call(
        functools.partial(exchange_kernel, experts),
        out_shape=(
            jax.ShapeDtypeStruct((rows, width), kind),
            jax.ShapeDtypeStruct((rows, width), kind),
            jax.ShapeDtypeStruct(gate_probs.shape[::-1], jnp.float32),
        ),
        in_specs=[hbm, hbm, vmem, vmem, hbm, hbm],
        out_specs=(vmem, vmem, vmem),
        scratch_shapes=[
            pltpu.VMEM((hidden_part, width), kind),
            pltpu.VMEM((hidden_part, width), kind),
            pltpu.VMEM((width, hidden_part), kind),
            pltpu.VMEM((width, hidden_part), kind),
            pltpu.VMEM((Z, C, Y, X, rows, wide), kind),
            pltpu.VMEM((Z, C, Y, X, rows, wide), kind),
            pltpu.VMEM((Z, Y, X, rows, wide), kind),
            pltpu.VMEM((Z, Y, X, rows, wide), kind),
            pltpu.VMEM((Z, 2, rows, wide), kind),
            pltpu.VMEM((Z, 2, rows, wide), kind),
            pltpu.VMEM((Z, rows, wide), kind),
            pltpu.VMEM((Z, rows, wide), kind),
            pltpu.VMEM((Z, rows, wide), kind),
            pltpu.SemaphoreType.DMA((4,)),
            pltpu.SemaphoreType.DMA((copies,)),
            pltpu.SemaphoreType.DMA((copies,)),
        ],
        compiler_params=pltpu.CompilerParams(
            collective_id=0, has_side_effects=True, vmem_limit_bytes=60 * 1024 * 1024
        ),
    )(tokens, cotangent, gate_probs.T, expert_ids.T, up_weight, down_weight)
    mixture, input_grad, gate_grad = pl.pallas_call(
        deliver_kernel,
        out_shape=tuple(jax.ShapeDtypeStruct(result.shape, result.dtype) for result in results),
        in_specs=[hbm] * len(results),
        out_specs=(hbm,) * len(results),
        scratch_shapes=[pltpu.SemaphoreType.DMA((len(results),))],
        compiler_params=pltpu.CompilerParams(vmem_limit_bytes=60 * 1024 * 1024),
    )(*results)
    return mixture, input_grad, gate_grad.T


def solution(mesh):
    small = dict(mesh.shape) == {"dp": Y, "expert": Z * X * C}
    placed = (
        P(("dp", "expert"), None),
        P(("dp", "expert"), None),
        P(("dp", "expert"), None),
        P(("dp", "expert"), None),
        P("expert", "dp", None),
        P("expert", "dp", None),
    )
    return jax.shard_map(
        token_shards if small else shards,
        mesh=mesh,
        in_specs=placed,
        out_specs=(P(("dp", "expert"), None), P(("dp", "expert"), None), P(("dp", "expert"), None)),
        check_vma=False,
    )
```

```python
import functools

import jax
import jax.numpy as jnp
from jax import lax
from jax.experimental import pallas as pl
from jax.experimental.pallas import tpu as pltpu
from jax.sharding import PartitionSpec as P


def broadcast(block, axis, owner):
    block = jnp.where(lax.axis_index(axis) == owner, block, jnp.zeros_like(block))
    return lax.psum(block, axis)


def expert_terms(row_block, up_piece, down_piece):
    model_width = row_block.shape[1] // 2
    features = row_block[:, :model_width]
    row_grads = row_block[:, model_width:]
    pre_act = jnp.einsum("rd,hd->rh", features, up_piece, preferred_element_type=jnp.float32)
    gating = jax.nn.sigmoid(pre_act)
    hidden = (pre_act * gating).astype(jnp.bfloat16)
    output_rows = jnp.dot(hidden, down_piece, preferred_element_type=jnp.float32)
    hidden_grad = jnp.einsum("rd,hd->rh", row_grads, down_piece, preferred_element_type=jnp.float32)
    act_grad = (hidden_grad * gating * (1.0 + pre_act * (1.0 - gating))).astype(jnp.bfloat16)
    input_rows = jnp.dot(act_grad, up_piece, preferred_element_type=jnp.float32)
    return jnp.concatenate([output_rows, input_rows], 1)


def spread(up_parts, down_parts, row_sets):
    model_width = up_parts.shape[2]
    initial = tuple(
        (jnp.zeros((row_block.shape[0], 2 * model_width), jnp.float32) for row_block in row_sets)
    )
    up_piece = lax.all_gather(up_parts, "dp", axis=1, tiled=True)
    down_piece = lax.all_gather(down_parts, "dp", axis=1, tiled=True)
    return tuple(
        (
            expert_terms(row_block, up_piece[member], down_piece[member])
            for member, (running, row_block) in enumerate(zip(initial, row_sets))
        )
    )


def shards(tokens, cotangent, gate_probs, expert_ids, up_weight, down_weight):
    tok_rows, model_width = tokens.shape
    top_count = expert_ids.shape[1]
    experts = lax.axis_size("expert")
    hot_rows = 9 * tok_rows // 16
    cold_total = experts - 1
    capacity = (tok_rows * top_count - hot_rows + cold_total - 1) // cold_total
    flat_ids = expert_ids.reshape(-1)
    slot_count = flat_ids.shape[0]
    one_hot = (flat_ids[:, None] == jnp.arange(experts, dtype=jnp.int32)[None, :]).astype(jnp.int32)
    hottest = jnp.argmax(jnp.sum(one_hot, 0))
    before = jnp.cumsum(one_hot, 0) - one_hot
    slot_rank = jnp.sum(before * one_hot, 1)
    slot_total = experts * capacity + hot_rows
    slot_index = jnp.where(
        flat_ids == hottest, experts * capacity + slot_rank, flat_ids * capacity + slot_rank
    )
    source_slot = (
        jnp.full((slot_total,), slot_count, jnp.int32)
        .at[slot_index]
        .set(jnp.arange(slot_count, dtype=jnp.int32))
    )
    source_row = source_slot // top_count
    payload = jnp.concatenate([tokens, cotangent], 1)
    padded_payload = jnp.concatenate([payload, jnp.zeros((1, 2 * model_width), payload.dtype)], 0)
    placed = padded_payload[source_row]
    outgoing = placed[: experts * capacity].reshape(experts, capacity, 2 * model_width)
    local_rows = placed[experts * capacity :]
    arrived = lax.all_to_all(outgoing, "expert", split_axis=0, concat_axis=0, tiled=True)
    arrived_rows = arrived.reshape(experts * capacity, 2 * model_width)
    shadow_up, shadow_down = (
        broadcast(up_weight[0], "expert", hottest),
        broadcast(down_weight[0], "expert", hottest),
    )
    (own_out,) = spread(up_weight, down_weight, [arrived_rows])
    (hot_out,) = spread(shadow_up[None], shadow_down[None], [local_rows])
    returning = own_out.astype(jnp.bfloat16).reshape(experts, capacity, 2 * model_width)
    came_back = lax.all_to_all(returning, "expert", split_axis=0, concat_axis=0, tiled=True)
    results = jnp.concatenate(
        [came_back.reshape(experts * capacity, 2 * model_width), hot_out.astype(jnp.bfloat16)], 0
    )
    per_slot = results[slot_index].astype(jnp.float32).reshape(tok_rows, top_count, 2 * model_width)
    scale = gate_probs[:, :, None]
    mixture = jnp.sum(scale * per_slot[:, :, :model_width], 1).astype(jnp.bfloat16)
    input_grad = jnp.sum(scale * per_slot[:, :, model_width:], 1).astype(jnp.bfloat16)
    gate_grad = jnp.sum(cotangent.astype(jnp.float32)[:, None, :] * per_slot[:, :, :model_width], 2)
    return (mixture, input_grad, gate_grad)


MESH = pl.DeviceIdType.MESH
LANES = 128
Z, Y, X, C = 4, 2, 2, 2


def exchange_kernel(
    experts,
    tokens_hbm, cotangent_hbm, gate_ref, ids_ref, up_hbm, down_hbm,
    mixture_ref, input_grad_ref, gate_grad_ref,
    up, down, up_turned, down_turned, gathered, partial, from_core, core_sum, from_first, first_sum, from_second, plane_sum, from_z,
    load_sem, send_sem, recv_sem,
):
    width = tokens_hbm.shape[1]
    near = LANES + width
    rows = tokens_hbm.shape[0]
    y, expert = lax.axis_index("dp"), lax.axis_index("expert")
    z = expert // (X * C)
    x = (expert // C) % X
    c = expert % C
    far_y, far_x, far_c = 1 - y, 1 - x, 1 - c

    def place(yy, zz, xx, cc):
        return (yy, (zz * X + xx) * C + cc)

    by_x, by_y, by_c = place(y, z, far_x, c), place(far_y, z, x, c), place(y, z, x, far_c)
    planes = [z, z + 1 - 2 * (z % 2), Z - 1 - z, (z + 2) % Z]
    inner = z % (Z - 1) > 0

    loads = [
        pltpu.make_async_copy(tokens_hbm, gathered.at[0, c, y, x, :, pl.ds(LANES, width)], load_sem.at[0]),
        pltpu.make_async_copy(cotangent_hbm, gathered.at[0, c, y, x, :, pl.ds(near, width)], load_sem.at[1]),
        pltpu.make_async_copy(up_hbm.at[0], up, load_sem.at[2]),
        pltpu.make_async_copy(down_hbm.at[0], down, load_sem.at[3]),
    ]
    for load in loads:
        load.start()

    barrier = pltpu.get_barrier_semaphore()
    partners = [by_x, by_y, by_c] + [place(y, planes[step], x, c) for step in range(1, Z)]
    for partner in partners:
        pl.semaphore_signal(barrier, inc=1, device_id=partner, device_id_type=MESH)

    slots = gate_ref.shape[0]
    names = lax.broadcasted_iota(jnp.int32, (LANES, rows), 0)
    weights = jnp.zeros((LANES, rows), jnp.float32)
    for k in range(slots):
        gate, chosen = gate_ref[k : k + 1, :], ids_ref[k : k + 1, :]
        high = gate.astype(jnp.bfloat16).astype(jnp.float32)
        weights += jnp.where(names == chosen, high, 0.0)
        weights += jnp.where(names == chosen + experts, gate - high, 0.0)
    square = (rows, rows)
    diagonal = lax.broadcasted_iota(jnp.int32, square, 0) == lax.broadcasted_iota(jnp.int32, square, 1)
    turned = lax.dot_general(
        jnp.where(diagonal, 1.0, 0.0).astype(jnp.bfloat16), weights.astype(jnp.bfloat16),
        (((1,), (1,)), ((), ())), preferred_element_type=jnp.float32,
    )
    gathered[0, c, y, x, :, :LANES] = turned.astype(jnp.bfloat16)
    loads[0].wait()
    loads[1].wait()
    pl.semaphore_wait(barrier, len(partners))

    started = []

    def prepare(src, dst, device):
        index = len(started)
        copy = pltpu.make_async_remote_copy(
            src_ref=src, dst_ref=dst, send_sem=send_sem.at[index], recv_sem=recv_sem.at[index],
            device_id=device, device_id_type=MESH,
        )
        started.append(copy)
        return copy

    def send(src, dst, device):
        copy = prepare(src, dst, device)
        copy.start()
        return copy

    first_cols, second_cols = pl.ds(0, near), pl.ds(near, width)
    pending = {}

    for j in range(1, Z):
        pending["z", j] = prepare(
            gathered.at[0, c, y, x], gathered.at[j, c, y, x], place(y, planes[j], x, c)
        )

    def send_plane(j):
        pending["z", j].start()

    def send_inner(j):
        @pl.when(inner)
        def _():
            pending["z", j].start()

    def send_outer(j):
        @pl.when(jnp.logical_not(inner))
        def _():
            pending["z", j].start()

    def gather_first(j):
        if j:
            pending["z", j].wait_recv()
        for name, cols, device in (("fa", first_cols, by_x), ("fb", second_cols, by_y)):
            ref = gathered.at[j, c, y, x, :, cols]
            pending[name, j] = send(ref, ref, device)

    def gather_second(j):
        pending["fa", j].wait_recv()
        ref = gathered.at[j, c, y, :, :, first_cols]
        pending["sa", j] = send(ref, ref, by_y)
        pending["fb", j].wait_recv()
        ref = gathered.at[j, c, :, x, :, second_cols]
        pending["sb", j] = send(ref, ref, by_x)

    def gather_core(j):
        for name, cols in (("a", first_cols), ("b", second_cols)):
            pending["s" + name, j].wait_recv()
            ref = gathered.at[j, c, :, :, :, cols]
            pending["c" + name, j] = send(ref, ref, by_c)

    def turn(index):
        loads[2 + index].wait()
        matrix, turned = ((up, up_turned), (down, down_turned))[index]
        block = min(256, width)
        for at in range(0, width, block):
            turned[at : at + block, :] = matrix[:, at : at + block].T

    def evaluate(j):
        pending["ca", j].wait_recv()
        group = C * Y * X * rows
        features = gathered[j, :, :, :, :, LANES:near].reshape(group, width)
        extra = gathered[j, :, :, :, :, :LANES].reshape(group, LANES).astype(jnp.float32)
        lanes = lax.broadcasted_iota(jnp.int32, (group, LANES), 1)
        mine = lanes == expert
        weight = jnp.sum(jnp.where(mine | (lanes == expert + experts), extra, 0.0), 1, keepdims=True)
        pre_act = jnp.dot(features, up_turned[...], preferred_element_type=jnp.float32)
        gating = jax.nn.sigmoid(pre_act)
        hidden = (pre_act * gating).astype(jnp.bfloat16)
        pending["cb", j].wait_recv()
        row_grads = gathered[j, :, :, :, :, near:].reshape(group, width)
        hidden_grad = jnp.dot(row_grads, down_turned[...], preferred_element_type=jnp.float32)
        act_grad = (hidden_grad * gating * (1.0 + pre_act * (1.0 - gating))).astype(jnp.bfloat16)
        products = jnp.sum(hidden.astype(jnp.float32) * hidden_grad, 1, keepdims=True)
        partial[j, :, :, :, :, :LANES] = (
            jnp.where(mine, products, 0.0).astype(jnp.bfloat16).reshape(C, Y, X, rows, LANES)
        )
        tile = min(512, width)
        for name, left, matrix, base, cols in (
            ("rca", hidden, down, LANES, first_cols), ("rcb", act_grad, up, near, second_cols)
        ):
            for at in range(0, width, tile):
                result = jnp.dot(left, matrix[:, at : at + tile], preferred_element_type=jnp.float32)
                partial[j, :, :, :, :, base + at : base + at + tile] = (
                    (result * weight).astype(jnp.bfloat16).reshape(C, Y, X, rows, tile)
                )
            pending[name, j] = send(
                partial.at[j, far_c, :, :, :, cols], from_core.at[j, :, :, :, cols], by_c
            )

    def add(one, other):
        return (one.astype(jnp.float32) + other.astype(jnp.float32)).astype(jnp.bfloat16)

    def reduce_first(j):
        pending["rca", j].wait_recv()
        core_sum[j, :, :, :, :near] = add(partial[j, c, :, :, :, :near], from_core[j, :, :, :, :near])
        pending["ra", j] = send(
            core_sum.at[j, far_y, :, :, first_cols], from_first.at[j, :, :, first_cols], by_y
        )
        pending["rcb", j].wait_recv()
        core_sum[j, :, :, :, near:] = add(partial[j, c, :, :, :, near:], from_core[j, :, :, :, near:])
        pending["rb", j] = send(
            core_sum.at[j, :, far_x, :, second_cols], from_first.at[j, :, :, second_cols], by_x
        )

    def reduce_second(j):
        pending["ra", j].wait_recv()
        first_sum[j, :, :, :near] = add(core_sum[j, y, :, :, :near], from_first[j, :, :, :near])
        pending["sra", j] = send(
            first_sum.at[j, far_x, :, first_cols], from_second.at[j, :, first_cols], by_x
        )
        pending["rb", j].wait_recv()
        for yy in range(Y):
            first_sum[j, yy, :, near:] = add(core_sum[j, yy, x, :, near:], from_first[j, yy, :, near:])
        pending["srb", j] = send(
            first_sum.at[j, far_y, :, second_cols], from_second.at[j, :, second_cols], by_y
        )

    def reduce_plane(j):
        for name, cols, kept in (
            ("a", slice(0, near), x), ("b", slice(near, near + width), y)
        ):
            pending["sr" + name, j].wait_recv()
            plane_sum[j, :, cols] = add(first_sum[j, kept, :, cols], from_second[j, :, cols])
            if j:
                part = first_cols if name == "a" else second_cols
                pending["rz" + name, j] = send(
                    plane_sum.at[j, :, part], from_z.at[j, :, part], place(y, planes[j], x, c)
                )

    order = (
        (send_plane, 1), (send_inner, 2), (gather_first, 0), (turn, 0), (gather_second, 0), (send_outer, 2),
        (turn, 1),
        (gather_first, 1), (send_plane, 3), (gather_core, 0), (gather_first, 2), (gather_second, 1),
        (evaluate, 0), (gather_second, 2), (gather_core, 1), (gather_first, 3), (evaluate, 1),
        (gather_core, 2), (gather_second, 3), (reduce_first, 1), (evaluate, 2),
        (gather_core, 3), (reduce_first, 2), (evaluate, 3), (reduce_second, 1),
        (reduce_first, 3), (reduce_second, 2), (reduce_plane, 1), (reduce_second, 3), (reduce_first, 0),
        (reduce_plane, 2), (reduce_plane, 3), (reduce_second, 0), (reduce_plane, 0),
    )
    for stage, j in order:
        stage(j)

    total = plane_sum[0].astype(jnp.float32)
    for j in range(1, Z):
        pending["rza", j].wait_recv()
        pending["rzb", j].wait_recv()
        total += from_z[j].astype(jnp.float32)
    mixture_ref[...] = total[:, LANES:near].astype(jnp.bfloat16)
    input_grad_ref[...] = total[:, near:].astype(jnp.bfloat16)
    per_expert = lax.dot_general(
        total[:, :LANES], jnp.where(diagonal, 1.0, 0.0), (((0,), (0,)), ((), ())),
        precision=lax.Precision.HIGHEST, preferred_element_type=jnp.float32,
    )
    for k in range(slots):
        gate_grad_ref[k : k + 1, :] = jnp.sum(
            jnp.where(names == ids_ref[k : k + 1, :], per_expert, 0.0), 0, keepdims=True
        )
    for copy in started:
        copy.wait_send()


def deliver_kernel(*refs):
    count = (len(refs) - 2) // 3
    load_sem, store_sem = refs[-2:]
    sources, targets, held = refs[:count], refs[count : 2 * count], refs[2 * count : 3 * count]
    loads = [pltpu.make_async_copy(sources[i], held[i], load_sem.at[i]) for i in range(count)]
    stores = [pltpu.make_async_copy(held[i], targets[i], store_sem.at[i]) for i in range(count)]
    for load in loads:
        load.start()
    for load, store in zip(loads, stores):
        load.wait()
        store.start()
    for store in stores:
        store.wait()


def token_shards(tokens, cotangent, gate_probs, expert_ids, up_weight, down_weight):
    rows, width = tokens.shape
    experts = lax.axis_size("expert")
    hidden_part = up_weight.shape[1]
    wide = LANES + 2 * width
    kind = jnp.bfloat16
    copies = 15 * Z
    vmem = pl.BlockSpec(memory_space=pltpu.VMEM)
    hbm = pl.BlockSpec(memory_space=pl.ANY)
    results = pl.pallas_call(
        functools.partial(exchange_kernel, experts),
        out_shape=(
            jax.ShapeDtypeStruct((rows, width), kind),
            jax.ShapeDtypeStruct((rows, width), kind),
            jax.ShapeDtypeStruct(gate_probs.shape[::-1], jnp.float32),
        ),
        in_specs=[hbm, hbm, vmem, vmem, hbm, hbm],
        out_specs=(vmem, vmem, vmem),
        scratch_shapes=[
            pltpu.VMEM((hidden_part, width), kind),
            pltpu.VMEM((hidden_part, width), kind),
            pltpu.VMEM((width, hidden_part), kind),
            pltpu.VMEM((width, hidden_part), kind),
            pltpu.VMEM((Z, C, Y, X, rows, wide), kind),
            pltpu.VMEM((Z, C, Y, X, rows, wide), kind),
            pltpu.VMEM((Z, Y, X, rows, wide), kind),
            pltpu.VMEM((Z, Y, X, rows, wide), kind),
            pltpu.VMEM((Z, 2, rows, wide), kind),
            pltpu.VMEM((Z, 2, rows, wide), kind),
            pltpu.VMEM((Z, rows, wide), kind),
            pltpu.VMEM((Z, rows, wide), kind),
            pltpu.VMEM((Z, rows, wide), kind),
            pltpu.SemaphoreType.DMA((4,)),
            pltpu.SemaphoreType.DMA((copies,)),
            pltpu.SemaphoreType.DMA((copies,)),
        ],
        compiler_params=pltpu.CompilerParams(
            collective_id=0, has_side_effects=True, vmem_limit_bytes=60 * 1024 * 1024
        ),
    )(tokens, cotangent, gate_probs.T, expert_ids.T, up_weight, down_weight)
    mixture, input_grad, gate_grad = pl.pallas_call(
        deliver_kernel,
        out_shape=tuple(jax.ShapeDtypeStruct(result.shape, result.dtype) for result in results),
        in_specs=[hbm] * len(results),
        out_specs=(hbm,) * len(results),
        scratch_shapes=[pltpu.VMEM(result.shape, result.dtype) for result in results]
        + [pltpu.SemaphoreType.DMA((len(results),))] * 2,
        compiler_params=pltpu.CompilerParams(vmem_limit_bytes=60 * 1024 * 1024),
    )(*results)
    return mixture, input_grad, gate_grad.T


def solution(mesh):
    small = dict(mesh.shape) == {"dp": Y, "expert": Z * X * C}
    placed = (
        P(("dp", "expert"), None),
        P(("dp", "expert"), None),
        P(("dp", "expert"), None),
        P(("dp", "expert"), None),
        P("expert", "dp", None),
        P("expert", "dp", None),
    )
    return jax.shard_map(
        token_shards if small else shards,
        mesh=mesh,
        in_specs=placed,
        out_specs=(P(("dp", "expert"), None), P(("dp", "expert"), None), P(("dp", "expert"), None)),
        check_vma=False,
    )
```
